32 devices in a mesh: dp: 4 (over x, core), seq: 8 (over z, y).
Axes of the slice: x: 2, y: 2, z: 4, core: 2. Of those that a mesh axis runs over, the one named last changes fastest.
Arguments:
- queries: bfloat16 [4, 2048, 4096], P('dp', 'seq'), may hold values from -51 to 51
- keys: bfloat16 [4, 2048, 512], P('dp', 'seq'), may hold values from -6 to 6
- values: bfloat16 [4, 2048, 512], P('dp', 'seq'), may hold values from -6 to 6
- targets: bfloat16 [4, 2048, 4096], P('dp', 'seq'), may hold values from -6 to 6
- q_map: bfloat16 [32, 128, 128], replicated, may hold values from -1.5 to 1.5
- k_map: bfloat16 [4, 128, 128], replicated, may hold values from -1.5 to 1.5
- doc_spans: int32 [4, 8], P('dp'), may hold values from 1 to 6, 16 in all within a row
Outputs:
- grad_q_map: float32 [32, 128, 128], replicated
- grad_k_map: float32 [4, 128, 128], replicated
The draws below stay inside these ranges and needn't reach their ends.
Inputs may be any that keep to these rules, and one draw needn't show every extreme that they name: `doc_spans`: each row sums to 16, and the longest document has exactly 6 blocks.
All inputs are finite; a program needn't handle non-finite values.
Results may differ from the reference program's by a relative error of at most 0.006.
The reference program's roundings to bfloat16 on the way count: a program that leaves them out, or rounds other values in their place, can miss the bound.
Values sent between devices are 32-bit elements; how exact they have to be, the bound alone decides.
No kernel may reach another device: no remote copies, remote signals or barrier semaphores. Data moves between devices by JAX's collectives and lax.ppermute only.
A program may use at most 128 MiB of HBM per device.

```python
import math
import jax
import jax.numpy as jnp
import numpy as np
from jax import lax

HQ = 32
HK = 4
HD = 128
SPAN = 128
NDOC = 8
BATCH = 4
LENGTH = 2048
SPANS = 16
MOST_DOC = 6


def draw_queries(key, part):
    shape = (BATCH, LENGTH, HQ * HD)
    base = jax.random.normal(jax.random.fold_in(key, 7), shape, jnp.float32)
    return jnp.clip(base, -6.0, 6.0).astype(jnp.bfloat16)


def block_scale(rng, dims, shards, least, top_value):
    loudness, own = 1.0, jax.random.fold_in(rng, 6)
    for position, blocks in shards:
        draws = jnp.exp(jax.random.uniform(jax.random.fold_in(own, position), (blocks,), jnp.float32, least / len(shards), top_value / len(shards)))
        loudness = loudness * jnp.repeat(draws, dims[position] // blocks).reshape([-1 if axis == position else 1 for axis in range(len(dims))])
    return loudness


def length_profile(number_of, total, limit, slope):
    weights = [(1 << 20) // math.isqrt(standing ** slope) + 1 for standing in range(2, number_of + 1)]
    surplus, given = total - limit - (number_of - 1), [1] * (number_of - 1)
    while surplus > 0:
        free = [i for i in range(number_of - 1) if given[i] < limit]
        whole, remaining = sum([weights[i] for i in free]), surplus
        for i in free:
            more = min(limit - given[i], max(1, remaining * weights[i] // whole), surplus)
            given[i] = given[i] + more
            surplus = surplus - more
    return np.array([limit] + given)


def ragged_sizes(own_key, number_of, total, limit, slope):
    if number_of == 2:
        one = jax.random.randint(own_key, (), max(1, total - limit), min(limit, total - 1) + 1)
        return jnp.stack([one, total - one])
    sizes = jnp.asarray(length_profile(number_of, total, limit, slope), jnp.int32)
    twos = (number_of - 1) // 2
    giver, sink = sizes[1:1 + 2 * twos:2], sizes[2:2 + 2 * twos:2]
    room = jnp.minimum(giver - 1, limit - sink)
    passed = jax.random.randint(jax.random.fold_in(own_key, 1), (twos,), 0, 1 << 20) % (room + 1)
    sizes = sizes.at[1:1 + 2 * twos:2].set(giver - passed).at[2:2 + 2 * twos:2].set(sink + passed)
    return sizes[jax.random.permutation(jax.random.fold_in(own_key, 2), number_of)]


def scatter_about(rng, dims, deviation, most, pieces=(), held_as=jnp.bfloat16):
    result = deviation * jax.random.normal(rng, dims, jnp.float32)
    if pieces:
        result = result * block_scale(rng, dims, pieces, -0.22, 0.18)
    return jnp.clip(result, -most, most).astype(held_as)


def setup_inputs(seed: int = 0) -> dict:
    streams_of = jax.random.split(jax.random.key(seed), 8)
    return {
        "queries": draw_queries(jax.random.fold_in(streams_of[7], 71), 0),
        "keys": scatter_about(streams_of[1], (BATCH, LENGTH, HK * HD), 1.0, 6.0, ((0, 4), (1, 8))),
        "values": scatter_about(streams_of[2], (BATCH, LENGTH, HK * HD), 1.0, 6.0, ((0, 4), (1, 8))),
        "targets": scatter_about(streams_of[3], (BATCH, LENGTH, HQ * HD), 1.0, 6.0, ((0, 4), (1, 8))),
        "q_map": scatter_about(streams_of[4], (HQ, HD, HD), 0.25, 1.5),
        "k_map": scatter_about(streams_of[5], (HK, HD, HD), 0.25, 1.5),
        "doc_spans": jax.vmap(lambda own: ragged_sizes(own, NDOC, SPANS, MOST_DOC, 2))(jax.random.split(streams_of[6], BATCH)).reshape((BATCH, NDOC)).astype(jnp.int32),
    }


def wide(array):
    return array.astype(jnp.float32)

def hedgehog(inputs, weight, form):
    mapped = jnp.einsum(form, wide(inputs), wide(weight), precision=lax.Precision.HIGHEST)
    upper = jax.nn.softmax(mapped, axis=-1)
    lower = jax.nn.softmax(-mapped, axis=-1)
    return (upper, lower, jnp.concatenate([upper, lower], axis=-1).astype(jnp.bfloat16))

def map_grad(upper, lower, grad, width):
    grad_up = grad[..., :width]
    grad_low = grad[..., width:]
    first = upper * (grad_up - lax.optimization_barrier(jnp.sum(upper * grad_up, -1, keepdims=True)))
    second = lower * (grad_low - lax.optimization_barrier(jnp.sum(lower * grad_low, -1, keepdims=True)))
    return (first - second).astype(jnp.bfloat16)

def product(form, left, right):
    return jnp.einsum(form, wide(left), wide(right), precision=lax.Precision.HIGHEST)

def span_middle(feat_q, feat_k, vals, tgt, state_b, norm_b, coef):
    size = feat_q.shape[1]
    causal = jnp.tril(jnp.ones((size, size), jnp.bool_))
    scores = product('ncxgf,nsxf->nxgcs', feat_q, feat_k)
    scores = jnp.where(causal, scores, 0.0)
    local_den = jnp.transpose(lax.optimization_barrier(jnp.sum(scores, -1)), (0, 3, 1, 2))
    numer = product('nxgcs,nsxd->ncxgd', scores.astype(jnp.bfloat16), vals)
    numer = numer + product('ncxgf,nxfd->ncxgd', feat_q, state_b)
    denom = local_den + product('ncxgf,nxf->ncxg', feat_q, norm_b)
    output = numer / denom[..., None]
    d_out = coef * (output - wide(tgt))
    d_numer = (d_out / denom[..., None]).astype(jnp.bfloat16)
    d_denom = -lax.optimization_barrier(jnp.sum(d_out * output, -1)) / denom
    pairs = product('ncxgd,nsxd->nxgcs', d_numer, vals)
    pairs = pairs + jnp.transpose(d_denom, (0, 2, 3, 1))[..., None]
    pairs = jnp.where(causal, pairs, 0.0).astype(jnp.bfloat16)
    d_feat_q = product('nxgcs,nsxf->ncxgf', pairs, feat_k)
    d_feat_q = d_feat_q + product('ncxgd,nxfd->ncxgf', d_numer, state_b)
    d_feat_q = d_feat_q + d_denom[..., None] * wide(norm_b)[:, None, :, None, :]
    back_state = product('ncxgf,ncxgd->nxfd', feat_q, d_numer)
    back_norm = product('ncxgf,ncxg->nxf', feat_q, d_denom)
    return (pairs, d_feat_q, back_state, back_norm)

def span_last(pairs, feat_q, vals, rstate_b, rnorm_b):
    d_feat_k = product('nxgcs,ncxgf->nsxf', pairs, feat_q)
    d_feat_k = d_feat_k + product('nsxd,nxfd->nsxf', vals, rstate_b)
    return d_feat_k + wide(rnorm_b)[:, None, :, :]

def one_sequence(items):
    queries, keys, values, targets, q_map, k_map, lengths = items
    hq = q_map.shape[0]
    hd = q_map.shape[1]
    hk = k_map.shape[0]
    group = hq // hk
    count = queries.shape[0] // SPAN
    coef = 2.0 / math.sqrt(BATCH * LENGTH * HD)
    q_heads = queries.reshape(count, SPAN, hq, hd)
    k_heads = keys.reshape(count, SPAN, hk, hd)
    vals = values.reshape(count, SPAN, hk, hd)
    tgt = targets.reshape(count, SPAN, hk, group, hd)
    q_up, q_low, feat_q = hedgehog(q_heads, q_map, 'ncxd,xde->ncxe')
    k_up, k_low, feat_k = hedgehog(k_heads, k_map, 'ncxd,xde->ncxe')
    feat_q = feat_q.reshape(count, SPAN, hk, group, 2 * hd)
    starts = jnp.cumsum(lengths) - lengths
    span_ids = jnp.arange(count, dtype=jnp.int32)
    opens = jnp.any(span_ids[:, None] == starts[None, :].astype(jnp.int32), axis=1)
    key_state = product('ncxf,ncxd->nxfd', feat_k, vals)
    key_norm = lax.optimization_barrier(jnp.sum(wide(feat_k), axis=1))

    def forward_step(carry, item):
        state, norm = carry
        add_state, add_norm, reset = item
        state = jnp.where(reset, 0.0, state)
        norm = jnp.where(reset, 0.0, norm)
        return ((state + add_state, norm + add_norm), (state, norm))
    zero_state = jnp.zeros(key_state.shape[1:], key_state.dtype)
    zero_norm = jnp.zeros(key_norm.shape[1:], key_norm.dtype)
    _, (state, norm) = lax.scan(forward_step, (zero_state, zero_norm), (key_state, key_norm, opens))
    pairs, d_feat_q, back_state, back_norm = span_middle(feat_q, feat_k, vals, tgt, state.astype(jnp.bfloat16), norm.astype(jnp.bfloat16), coef)

    def reverse_step(carry, item):
        state_r, norm_r = carry
        add_state, add_norm, reset = item
        out = (state_r, norm_r)
        state_r = jnp.where(reset, 0.0, state_r + add_state)
        norm_r = jnp.where(reset, 0.0, norm_r + add_norm)
        return ((state_r, norm_r), out)
    zero_rstate = jnp.zeros(back_state.shape[1:], back_state.dtype)
    zero_rnorm = jnp.zeros(back_norm.shape[1:], back_norm.dtype)
    _, (rstate, rnorm) = lax.scan(reverse_step, (zero_rstate, zero_rnorm), (back_state, back_norm, opens), reverse=True)
    d_feat_k = span_last(pairs, feat_q, vals, rstate.astype(jnp.bfloat16), rnorm.astype(jnp.bfloat16))
    du_q = map_grad(q_up, q_low, d_feat_q.reshape(count, SPAN, hq, 2 * hd), hd)
    du_k = map_grad(k_up, k_low, d_feat_k, hd)
    grad_q = product('ncxd,ncxe->xde', q_heads, du_q)
    grad_k = product('ncxd,ncxe->xde', k_heads, du_k)
    return (grad_q, grad_k)

def reference(queries, keys, values, targets, q_map, k_map, doc_spans):
    batch = queries.shape[0]
    q_maps = jnp.broadcast_to(q_map[None], (batch,) + q_map.shape)
    k_maps = jnp.broadcast_to(k_map[None], (batch,) + k_map.shape)
    grad_q, grad_k = lax.map(one_sequence, (queries, keys, values, targets, q_maps, k_maps, doc_spans))
    return (lax.optimization_barrier(jnp.sum(grad_q, axis=0)), lax.optimization_barrier(jnp.sum(grad_k, axis=0)))
```

```python
import functools
import math

import jax
import jax.numpy as jnp
from jax import lax
from jax.experimental import pallas as pl
from jax.experimental.pallas import tpu as pltpu
from jax.sharding import PartitionSpec as P

SPAN = 128
PAD = 8
F32 = jnp.float32
BF16 = jnp.bfloat16
NN = (((1,), (0,)), ((), ()))
NT = (((1,), (1,)), ((), ()))
TN = (((0,), (0,)), ((), ()))


def dot(left, right, dims):
    return lax.dot_general(left, right, dims, preferred_element_type=F32)


def bounds(spans_ref, block):
    start, end, place = jnp.int32(0), jnp.int32(0), jnp.int32(0)
    for d in range(spans_ref.shape[1]):
        after = place + spans_ref[0, d]
        inside = jnp.logical_and(block >= place, block < after)
        start = jnp.where(inside, place, start)
        end = jnp.where(inside, after, end)
        place = after
    return start, end


def flag(condition):
    return jnp.where(condition, jnp.float32(1.0), jnp.float32(0.0))


def soft_pair(mapped):
    up = jnp.exp(mapped - jnp.max(mapped, -1, keepdims=True))
    low = jnp.exp(jnp.min(mapped, -1, keepdims=True) - mapped)
    up = up * (1.0 / jnp.sum(up, -1, keepdims=True))
    low = low * (1.0 / jnp.sum(low, -1, keepdims=True))
    return up, low


def map_grad(up, low, grad_up, grad_low):
    first = up * (grad_up - jnp.sum(up * grad_up, -1, keepdims=True))
    second = low * (grad_low - jnp.sum(low * grad_low, -1, keepdims=True))
    return (first - second).astype(BF16)


def key_kernel(count, spans_ref, k_ref, v_ref, w_ref, feat_ref, block_ref, *tail_refs):
    width = w_ref.shape[-1]
    heads = w_ref.shape[0]
    first = lax.axis_index("seq") * count
    starts = [bounds(spans_ref, first + c)[0] for c in range(count)]
    for i in range(heads):
        cols = slice(i * width, (i + 1) * width)
        up, low = soft_pair(dot(k_ref[:, cols], w_ref[i], NN))
        feat = jnp.concatenate([up, low], axis=-1).astype(BF16)
        feat_ref[i] = feat
        tail = None
        for c in range(count):
            rows = slice(c * SPAN, (c + 1) * SPAN)
            state = dot(v_ref[rows, cols], feat[rows], TN)
            norm = jnp.sum(feat[rows].astype(F32), axis=0, keepdims=True)
            norm = jnp.broadcast_to(norm, (PAD, norm.shape[1]))
            both = jnp.concatenate([state, norm], axis=0)
            block_ref[i, c] = both
            part = flag(starts[c] == starts[count - 1]) * both
            tail = part if tail is None else tail + part
        tail_refs[i][...] = tail


def join_kernel(count, hop, reverse, spans_ref, own_ref, came_ref, out_ref):
    place = lax.axis_index("seq")
    if reverse:
        _, end = bounds(spans_ref, place * count)
        keep = flag(end > (place + hop) * count)
    else:
        start, _ = bounds(spans_ref, place * count + count - 1)
        keep = flag(start < (place - hop + 1) * count)
    out_ref[...] = own_ref[...] + keep * came_ref[...]


def middle_kernel(count, group, hops, coef, *refs):
    spans_ref, q_ref, t_ref, v_ref, feat_ref, w_ref, block_ref = refs[:7]
    came = refs[7 : 7 + hops]
    gq_ref, head_ref, back_ref, part_ref = refs[7 + hops : 11 + hops]
    width = w_ref.shape[-1]
    c = pl.program_id(0)
    place = lax.axis_index("seq")
    first = place * count
    start_first, _ = bounds(spans_ref, first)
    start, _ = bounds(spans_ref, first + c)
    state = None
    for k in range(hops):
        near = start_first < (place - (1 << k) + 1) * count
        part = flag(jnp.logical_and(near, start < first)) * came[k][...]
        state = part if state is None else state + part
    for e in range(count - 1):
        state = state + flag(jnp.logical_and(e < c, start <= first + e)) * block_ref[e]
    norm = state[SPAN : SPAN + 1].astype(BF16).astype(F32)
    mat = jnp.concatenate([feat_ref[...], state[:SPAN].astype(BF16)], axis=0)
    vals = v_ref[...]
    qs = [q_ref[:, h * width : (h + 1) * width] for h in range(group)]
    mapped = jnp.concatenate([dot(qs[h], w_ref[h], NN) for h in range(group)], axis=0)
    up, low = soft_pair(mapped)
    feat = jnp.concatenate([up, low], axis=-1).astype(BF16)
    wide = feat.astype(F32)
    both = dot(feat, mat, NT)
    rows = group * SPAN
    row = lax.broadcasted_iota(jnp.int32, (rows, SPAN), 0) & (SPAN - 1)
    causal = row >= lax.broadcasted_iota(jnp.int32, (rows, SPAN), 1)
    scores = jnp.where(causal, both[:, :SPAN], 0.0)
    weighed = wide * norm
    denom = jnp.sum(scores + weighed[:, :width] + weighed[:, width:], -1, keepdims=True)
    numer = dot(scores.astype(BF16), vals, NN) + both[:, SPAN:]
    inverse = 1.0 / denom
    output = numer * inverse
    tgt = jnp.concatenate([t_ref[:, h * width : (h + 1) * width] for h in range(group)], axis=0)
    d_out = coef * (output - tgt.astype(F32))
    d_numer = (d_out * inverse).astype(BF16)
    d_denom = -jnp.sum(d_out * output, -1, keepdims=True) * inverse
    pairs = jnp.where(causal, dot(d_numer, vals, NT) + d_denom, 0.0).astype(BF16)
    d_feat = dot(jnp.concatenate([pairs, d_numer], axis=-1), mat, NN) + d_denom * norm
    crossed = dot(jnp.concatenate([d_numer, pairs], axis=-1), feat, TN)
    back_norm = jnp.sum(wide * d_denom, axis=0, keepdims=True)
    back_norm = jnp.broadcast_to(back_norm, (PAD, back_norm.shape[1]))
    back = jnp.concatenate([crossed[:SPAN], back_norm], axis=0)
    back_ref[...] = back
    part_ref[...] = crossed[SPAN:]
    d_map = map_grad(up, low, d_feat[:, :width], d_feat[:, width:])
    grads = [dot(qs[h], d_map[h * SPAN : (h + 1) * SPAN], TN) for h in range(group)]
    mine = flag(start == start_first) * back

    @pl.when(c == 0)
    def _():
        head_ref[...] = mine
        for h in range(group):
            gq_ref[h] = grads[h]

    @pl.when(c > 0)
    def _():
        head_ref[...] += mine
        for h in range(group):
            gq_ref[h] += grads[h]


def last_kernel(count, hops, *refs):
    spans_ref, k_ref, v_ref, w_ref, back_ref, part_ref = refs[:6]
    came = refs[6 : 6 + hops]
    gk_ref = refs[6 + hops]
    width = w_ref.shape[-1]
    place = lax.axis_index("seq")
    first = place * count
    _, end_last = bounds(spans_ref, first + count - 1)
    keys = k_ref[...]
    up, low = soft_pair(dot(keys, w_ref[...], NN))
    grads = []
    for c in range(count):
        _, end = bounds(spans_ref, first + c)
        state = None
        for k in range(hops):
            near = end_last > (place + (1 << k)) * count
            part = flag(jnp.logical_and(near, end > first + count)) * came[k][...]
            state = part if state is None else state + part
        for e in range(c + 1, count):
            state = state + flag(end > first + e) * back_ref[e]
        norm = state[SPAN : SPAN + 1].astype(BF16).astype(F32)
        grad = part_ref[c] + dot(v_ref[c * SPAN : (c + 1) * SPAN], state[:SPAN].astype(BF16), NN)
        grads.append(grad + norm)
    d_feat = jnp.concatenate(grads, axis=0)
    d_map = map_grad(up, low, d_feat[:, :width], d_feat[:, width:])
    gk_ref[...] = dot(keys, d_map, TN)


def cost(flops, moved):
    return pl.CostEstimate(flops=int(flops), bytes_accessed=int(moved), transcendentals=0)


SMEM = pl.BlockSpec(memory_space=pltpu.SMEM)
LIMIT = 48 << 20


def whole_call(body, out_shape, n_vmem, flops, *args):
    moved = sum(a.size * a.dtype.itemsize for a in args)
    return pl.pallas_call(
        body,
        out_shape=out_shape,
        in_specs=[SMEM] + [pl.BlockSpec(memory_space=pltpu.VMEM)] * n_vmem,
        compiler_params=pltpu.CompilerParams(vmem_limit_bytes=LIMIT),
        cost_estimate=cost(flops, moved),
    )(*args)


def swap(x, axis, size, bit):
    return lax.ppermute(x, axis, [(i, i ^ (1 << bit)) for i in range(size)])


def sum_all(x, steps):
    for axis, size, bit in steps:
        mine = (lax.axis_index(axis) >> bit) & 1
        pair = x.reshape(2, x.shape[0] // 2, x.shape[1])
        send = lax.dynamic_index_in_dim(pair, 1 - mine, 0, False)
        keep = lax.dynamic_index_in_dim(pair, mine, 0, False)
        x = keep + swap(send, axis, size, bit)
    for axis, size, bit in reversed(steps):
        mine = (lax.axis_index(axis) >> bit) & 1
        came = swap(x, axis, size, bit)
        x = jnp.concatenate([jnp.where(mine == 0, x, came), jnp.where(mine == 0, came, x)], axis=0)
    return x


def solution(mesh):
    n_dp, n_seq = mesh.shape["dp"], mesh.shape["seq"]

    def shards(queries, keys, values, targets, q_map, k_map, doc_spans):
        hq, hd = q_map.shape[0], q_map.shape[1]
        hk = k_map.shape[0]
        group = hq // hk
        rows = queries.shape[1]
        count = rows // SPAN
        feats = 2 * hd
        tall = SPAN + PAD
        coef = 2.0 / math.sqrt(n_dp * n_seq * rows * hd)
        most = (3 * n_seq * count) // 8
        before = min(n_seq - 1, -(-(most - 1) // count))
        hops = max(1, before.bit_length())
        q2, t2 = queries[0], targets[0]
        k2, v2 = keys[0], values[0]
        state_t = jax.ShapeDtypeStruct((tall, feats), F32)

        out = whole_call(
            functools.partial(key_kernel, count),
            [
                jax.ShapeDtypeStruct((hk, rows, feats), BF16),
                jax.ShapeDtypeStruct((hk, count, tall, feats), F32),
            ]
            + [state_t] * hk,
            3,
            2 * hk * rows * hd * (hd + feats),
            doc_spans,
            k2,
            v2,
            k_map,
        )
        feat_k, blocks, tails = out[0], out[1], out[2:]

        def exchange(own, reverse):
            came = []
            for k in range(hops):
                hop = 1 << k
                if reverse:
                    perm = [(i, i - hop) for i in range(hop, n_seq)]
                else:
                    perm = [(i, i + hop) for i in range(n_seq - hop)]
                got = lax.ppermute(own, "seq", perm)
                came.append(got)
                if k < hops - 1:
                    own = whole_call(
                        functools.partial(join_kernel, count, hop, reverse),
                        state_t,
                        2,
                        own.size,
                        doc_spans,
                        own,
                        got,
                    )
            return came

        def middle(i, came):
            block = lambda shape, index: pl.BlockSpec(shape, index)
            state = block((tall, feats), lambda c: (0, 0))
            flops = 2 * group * rows * hd * (6 * feats + 3 * hd)
            return pl.pallas_call(
                functools.partial(middle_kernel, count, group, hops, coef),
                grid=(count,),
                in_specs=[
                    SMEM,
                    block((SPAN, group * hd), lambda c: (c, i)),
                    block((SPAN, group * hd), lambda c: (c, i)),
                    block((SPAN, hd), lambda c: (c, i)),
                    block((None, SPAN, feats), lambda c: (i, c, 0)),
                    block((group, hd, hd), lambda c: (i, 0, 0)),
                    block((None, count, tall, feats), lambda c: (i, 0, 0, 0)),
                ]
                + [state] * hops,
                out_specs=[
                    block((group, hd, hd), lambda c: (0, 0, 0)),
                    state,
                    block((None, tall, feats), lambda c: (c, 0, 0)),
                    block((None, SPAN, feats), lambda c: (c, 0, 0)),
                ],
                out_shape=[
                    jax.ShapeDtypeStruct((group, hd, hd), F32),
                    state_t,
                    jax.ShapeDtypeStruct((count, tall, feats), F32),
                    jax.ShapeDtypeStruct((count, SPAN, feats), F32),
                ],
                compiler_params=pltpu.CompilerParams(vmem_limit_bytes=LIMIT),
                cost_estimate=cost(flops, 4 * rows * group * hd),
            )(doc_spans, q2, t2, v2, feat_k, q_map, blocks, *came)

        def last(i, back, part, came):
            block = lambda shape, index: pl.BlockSpec(shape, index)
            return pl.pallas_call(
                functools.partial(last_kernel, count, hops),
                grid=(1,),
                in_specs=[
                    SMEM,
                    block((rows, hd), lambda c: (0, i)),
                    block((rows, hd), lambda c: (0, i)),
                    block((None, hd, hd), lambda c: (i, 0, 0)),
                    block((count, tall, feats), lambda c: (0, 0, 0)),
                    block((count, SPAN, feats), lambda c: (0, 0, 0)),
                ]
                + [block((tall, feats), lambda c: (0, 0))] * hops,
                out_specs=block((hd, hd), lambda c: (0, 0)),
                out_shape=jax.ShapeDtypeStruct((hd, hd), F32),
                compiler_params=pltpu.CompilerParams(vmem_limit_bytes=LIMIT),
                cost_estimate=cost(2 * rows * hd * 2 * feats, rows * feats * 4),
            )(doc_spans, k2, v2, k_map, back, part, *came)

        steps = [("dp", n_dp, b) for b in range(n_dp.bit_length() - 1)]
        steps += [("seq", n_seq, b) for b in range(n_seq.bit_length() - 1)]
        came = [exchange(tails[i], False) for i in range(hk)]
        mids = [middle(i, came[i]) for i in range(hk)]
        backs = [exchange(mids[i][1], True) for i in range(hk)]
        gq = [sum_all(mids[i][0].reshape(-1, hd), steps) for i in range(hk)]
        gk = [last(i, mids[i][2], mids[i][3], backs[i]) for i in range(hk)]
        grad_q = jnp.concatenate(gq, axis=0).reshape(hq, hd, hd)
        grad_k = sum_all(jnp.concatenate(gk, axis=0), steps).reshape(hk, hd, hd)
        return grad_q, grad_k

    in_specs = (
        P("dp", "seq", None),
        P("dp", "seq", None),
        P("dp", "seq", None),
        P("dp", "seq", None),
        P(),
        P(),
        P("dp", None),
    )
    return jax.shard_map(
        shards, mesh=mesh, in_specs=in_specs, out_specs=(P(), P()), check_vma=False
    )
```

```python
import functools
import math

import jax
import jax.numpy as jnp
from jax import lax
from jax.experimental import pallas as pl
from jax.experimental.pallas import tpu as pltpu
from jax.sharding import PartitionSpec as P

SPAN = 128
PAD = 8
WHOLE = 256
F32 = jnp.float32
BF16 = jnp.bfloat16
NN = (((1,), (0,)), ((), ()))
NT = (((1,), (1,)), ((), ()))
TN = (((0,), (0,)), ((), ()))


def dot(left, right, dims):
    return lax.dot_general(left, right, dims, preferred_element_type=F32)


def bounds(spans_ref, block):
    start, end, place = jnp.int32(0), jnp.int32(0), jnp.int32(0)
    for d in range(spans_ref.shape[1]):
        after = place + spans_ref[0, d]
        inside = jnp.logical_and(block >= place, block < after)
        start = jnp.where(inside, place, start)
        end = jnp.where(inside, after, end)
        place = after
    return start, end


def flag(condition):
    return jnp.where(condition, jnp.float32(1.0), jnp.float32(0.0))


def soft_pair(mapped):
    up = jnp.exp(mapped - jnp.max(mapped, -1, keepdims=True))
    low = jnp.exp(jnp.min(mapped, -1, keepdims=True) - mapped)
    up = up * (1.0 / jnp.sum(up, -1, keepdims=True))
    low = low * (1.0 / jnp.sum(low, -1, keepdims=True))
    return up, low


def map_grad(up, low, grad_up, grad_low):
    first = up * (grad_up - jnp.sum(up * grad_up, -1, keepdims=True))
    second = low * (grad_low - jnp.sum(low * grad_low, -1, keepdims=True))
    return (first - second).astype(BF16)


def key_kernel(count, parts, spans_ref, k_ref, v_ref, w_ref, feat_ref, block_ref, *tail_refs):
    head = pl.program_id(0)
    first = lax.axis_index("seq") * count
    starts = [bounds(spans_ref, first + c)[0] for c in range(count)]
    up, low = soft_pair(dot(k_ref[...], w_ref[...], NN))
    feat = jnp.concatenate([up, low], axis=-1).astype(BF16)
    feat_ref[...] = feat
    tail = None
    for c in range(count):
        rows = slice(c * SPAN, (c + 1) * SPAN)
        state = dot(v_ref[rows], feat[rows], TN)
        norm = jnp.sum(feat[rows].astype(F32), axis=0, keepdims=True)
        norm = jnp.broadcast_to(norm, (PAD, norm.shape[1]))
        both = jnp.concatenate([state, norm], axis=0)
        block_ref[c] = both
        part = flag(starts[c] == starts[count - 1]) * both
        tail = part if tail is None else tail + part
    for (low_head, high_head), tail_ref in zip(parts, tail_refs):

        @pl.when(jnp.logical_and(head >= low_head, head < high_head))
        def _():
            tail_ref[...] = tail


def join_kernel(count, hop, reverse, spans_ref, own_ref, came_ref, out_ref):
    place = lax.axis_index("seq")
    if reverse:
        _, end = bounds(spans_ref, place * count)
        keep = flag(end > (place + hop) * count)
    else:
        start, _ = bounds(spans_ref, place * count + count - 1)
        keep = flag(start < (place - hop + 1) * count)
    out_ref[...] = own_ref[...] + keep * came_ref[...]


def middle_kernel(count, group, hops, coef, *refs):
    spans_ref, q_ref, t_ref, v_ref, feat_ref, w_ref, block_ref = refs[:7]
    came = refs[7 : 7 + hops]
    keep_ref, send_ref, head_ref, back_ref, part_ref = refs[7 + hops : 12 + hops]
    width = w_ref.shape[-1]
    c = pl.program_id(1)
    place = lax.axis_index("seq")
    first = place * count
    start_first, _ = bounds(spans_ref, first)
    start, _ = bounds(spans_ref, first + c)
    state = None
    for k in range(hops):
        near = start_first < (place - (1 << k) + 1) * count
        part = flag(jnp.logical_and(near, start < first)) * came[k][...]
        state = part if state is None else state + part
    for e in range(count - 1):
        state = state + flag(jnp.logical_and(e < c, start <= first + e)) * block_ref[e]
    norm = state[SPAN : SPAN + 1].astype(BF16).astype(F32)
    mat = jnp.concatenate([feat_ref[...], state[:SPAN].astype(BF16)], axis=0)
    vals = v_ref[...]
    qs = [q_ref[:, h * width : (h + 1) * width] for h in range(group)]
    mapped = jnp.concatenate([dot(qs[h], w_ref[h], NN) for h in range(group)], axis=0)
    up, low = soft_pair(mapped)
    feat = jnp.concatenate([up, low], axis=-1).astype(BF16)
    wide = feat.astype(F32)
    both = dot(feat, mat, NT)
    rows = group * SPAN
    row = lax.broadcasted_iota(jnp.int32, (rows, SPAN), 0) & (SPAN - 1)
    causal = row >= lax.broadcasted_iota(jnp.int32, (rows, SPAN), 1)
    scores = jnp.where(causal, both[:, :SPAN], 0.0)
    weighed = wide * norm
    denom = jnp.sum(scores + weighed[:, :width] + weighed[:, width:], -1, keepdims=True)
    numer = dot(scores.astype(BF16), vals, NN) + both[:, SPAN:]
    inverse = 1.0 / denom
    output = numer * inverse
    tgt = jnp.concatenate([t_ref[:, h * width : (h + 1) * width] for h in range(group)], axis=0)
    d_out = coef * (output - tgt.astype(F32))
    d_numer = (d_out * inverse).astype(BF16)
    d_denom = -jnp.sum(d_out * output, -1, keepdims=True) * inverse
    pairs = jnp.where(causal, dot(d_numer, vals, NT) + d_denom, 0.0).astype(BF16)
    d_feat = dot(jnp.concatenate([pairs, d_numer], axis=-1), mat, NN) + d_denom * norm
    crossed = dot(jnp.concatenate([d_numer, pairs], axis=-1), feat, TN)
    back_norm = jnp.sum(wide * d_denom, axis=0, keepdims=True)
    back_norm = jnp.broadcast_to(back_norm, (PAD, back_norm.shape[1]))
    back = jnp.concatenate([crossed[:SPAN], back_norm], axis=0)
    back_ref[...] = back
    part_ref[...] = crossed[SPAN:]
    d_map = map_grad(up, low, d_feat[:, :width], d_feat[:, width:])
    grads = [dot(qs[h], d_map[h * SPAN : (h + 1) * SPAN], TN) for h in range(group)]
    mine = flag(start == start_first) * back
    half = group // 2
    core = lax.axis_index("dp") & 1

    def put(ref, base, add):
        for h in range(half):
            grad = jnp.where(core == 0, grads[base + h], grads[half - base + h])
            rows = slice(h * width, (h + 1) * width)
            ref[rows] = ref[rows] + grad if add else grad

    @pl.when(c == 0)
    def _():
        head_ref[...] = mine
        put(keep_ref, 0, False)
        put(send_ref, half, False)

    @pl.when(c > 0)
    def _():
        head_ref[...] += mine
        put(keep_ref, 0, True)
        put(send_ref, half, True)


def last_kernel(count, hops, *refs):
    spans_ref, k_ref, v_ref, w_ref, back_ref, part_ref = refs[:6]
    came = refs[6 : 6 + hops]
    gk_ref = refs[6 + hops]
    width = w_ref.shape[-1]
    place = lax.axis_index("seq")
    first = place * count
    _, end_last = bounds(spans_ref, first + count - 1)
    keys = k_ref[...]
    up, low = soft_pair(dot(keys, w_ref[...], NN))
    grads = []
    for c in range(count):
        _, end = bounds(spans_ref, first + c)
        state = None
        for k in range(hops):
            near = end_last > (place + (1 << k)) * count
            part = flag(jnp.logical_and(near, end > first + count)) * came[k][...]
            state = part if state is None else state + part
        for e in range(c + 1, count):
            state = state + flag(end > first + e) * back_ref[e]
        norm = state[SPAN : SPAN + 1].astype(BF16).astype(F32)
        grad = part_ref[c] + dot(v_ref[c * SPAN : (c + 1) * SPAN], state[:SPAN].astype(BF16), NN)
        grads.append(grad + norm)
    d_feat = jnp.concatenate(grads, axis=0)
    d_map = map_grad(up, low, d_feat[:, :width], d_feat[:, width:])
    gk_ref[...] = dot(keys, d_map, TN)


def cost(flops, moved):
    return pl.CostEstimate(flops=int(flops), bytes_accessed=int(moved), transcendentals=0)


SMEM = pl.BlockSpec(memory_space=pltpu.SMEM)
LIMIT = 48 << 20
LATE = 400


def whole_call(body, out_shape, n_vmem, flops, *args):
    moved = sum(a.size * a.dtype.itemsize for a in args)
    return pl.pallas_call(
        body,
        out_shape=out_shape,
        in_specs=[SMEM] + [pl.BlockSpec(memory_space=pltpu.VMEM)] * n_vmem,
        compiler_params=pltpu.CompilerParams(vmem_limit_bytes=LIMIT),
        cost_estimate=cost(flops, moved),
    )(*args)


def index_in(stage):
    place = jnp.int32(0)
    for k, (axis, bit) in enumerate(stage):
        place = place + (((lax.axis_index(axis) >> bit) & 1) << k)
    return place


def split_kernel(stage, layout, *refs):
    pieces = 1 << len(stage)
    outs = refs[len(refs) - pieces :]
    mine = index_in(stage)
    for m, out in enumerate(outs):
        at, used = 0, 0
        for addends, rows in layout:
            size = rows // pieces
            start = 0 if pieces == 1 else pl.multiple_of((mine ^ m) * size, PAD)
            total = refs[used][pl.ds(start, size), :]
            for ref in refs[used + 1 : used + addends]:
                total = total + ref[pl.ds(start, size), :]
            out[at : at + size] = total
            at, used = at + size, used + addends


def join_pieces_kernel(stage, layout, *refs):
    pieces = 1 << len(stage)
    out = refs[pieces]
    mine = index_in(stage)
    for m in range(pieces):
        at, base = 0, 0
        for _, rows in layout:
            size = rows // pieces
            start = pl.multiple_of(base + (mine ^ m) * size, PAD)
            out[pl.ds(start, size), :] = refs[m][at : at + size]
            at, base = at + size, base + rows


def plain_call(body, out_shape, *args):
    moved = 2 * sum(a.size * a.dtype.itemsize for a in args)
    return pl.pallas_call(
        body,
        out_shape=out_shape,
        in_specs=[pl.BlockSpec(memory_space=pltpu.VMEM)] * len(args),
        compiler_params=pltpu.CompilerParams(vmem_limit_bytes=LIMIT),
        cost_estimate=cost(moved, moved),
    )(*args)


def rows_of(rows, width):
    return jax.ShapeDtypeStruct((rows, width), F32)


class Summer:
    def __init__(self, n_dp, n_seq):
        self.n_dp, self.n_seq = n_dp, n_seq
        bits = [("dp", b) for b in range(1, n_dp.bit_length() - 1)]
        seq = [("seq", b) for b in range(n_seq.bit_length() - 1)]
        rest = bits[:1] + seq[:1] + seq[1:] + bits[1:]
        self.core = [("dp", 0)]
        self.stages = [rest[k : k + 2] for k in range(0, len(rest), 2)]

    def send(self, x, stage, mask):
        d_mask = sum(1 << b for k, (a, b) in enumerate(stage) if a == "dp" and mask >> k & 1)
        s_mask = sum(1 << b for k, (a, b) in enumerate(stage) if a == "seq" and mask >> k & 1)
        perm = [
            (d * self.n_seq + s, (d ^ d_mask) * self.n_seq + (s ^ s_mask))
            for d in range(self.n_dp)
            for s in range(self.n_seq)
        ]
        return lax.ppermute(x, ("dp", "seq"), perm)

    def split(self, groups, stage):
        pieces = 1 << len(stage)
        layout = [(len(g), g[0].shape[0]) for g in groups]
        size = sum(rows for _, rows in layout) // pieces
        width = groups[0][0].shape[1]
        out = plain_call(
            functools.partial(split_kernel, stage, layout),
            [rows_of(size, width)] * pieces,
            *[a for g in groups for a in g],
        )
        return out, layout

    def join(self, x, stage, layout):
        came = [x] + [self.send(x, stage, m) for m in range(1, 1 << len(stage))]
        total = sum(rows for _, rows in layout)
        return plain_call(
            functools.partial(join_pieces_kernel, stage, layout), rows_of(total, x.shape[1]), *came
        )

    def __call__(self, groups, stages):
        done = []
        for stage in stages:
            rows = [g[0].shape[0] for g in groups]
            if sum(rows) > WHOLE and min(rows) >> len(stage) >= PAD:
                out, layout = self.split(groups, stage)
                done.append((stage, layout))
            else:
                whole, _ = self.split(groups, [])
                out = [whole[0]] * (1 << len(stage))
            groups = [[out[0]] + [self.send(out[m], stage, m) for m in range(1, len(out))]]
        x = self.split(groups, [])[0][0]
        for stage, layout in reversed(done):
            x = self.join(x, stage, layout)
        return x


def assemble_kernel(parts, half, *refs):
    out = refs[-1]
    mine = lax.axis_index("dp") & 1
    for p, (low, high) in enumerate(parts):
        for side in range(2):
            for i in range(low, high):
                start = pl.multiple_of((2 * i + (mine ^ side)) * half, PAD)
                rows = slice((i - low) * half, (i - low + 1) * half)
                out[pl.ds(start, half), :] = refs[2 * p + side][rows]


def solution(mesh):
    n_dp, n_seq = mesh.shape["dp"], mesh.shape["seq"]

    def shards(queries, keys, values, targets, q_map, k_map, doc_spans):
        hq, hd = q_map.shape[0], q_map.shape[1]
        hk = k_map.shape[0]
        group = hq // hk
        rows = queries.shape[1]
        count = rows // SPAN
        feats = 2 * hd
        tall = SPAN + PAD
        coef = 2.0 / math.sqrt(n_dp * n_seq * rows * hd)
        most = (3 * n_seq * count) // 8
        before = min(n_seq - 1, -(-(most - 1) // count))
        hops = max(1, before.bit_length())
        q2, t2 = queries[0], targets[0]
        k2, v2 = keys[0], values[0]
        state_t = jax.ShapeDtypeStruct((tall, feats), F32)

        block = lambda shape, index: pl.BlockSpec(shape, index)
        parts = [(0, hk // 2), (hk // 2, hk)]
        tail_specs = [
            block((tall, feats), lambda i, lo=lo, hi=hi: (jnp.clip(i, lo, hi - 1) - lo, 0))
            for lo, hi in parts
        ]
        out = pl.pallas_call(
            functools.partial(key_kernel, count, parts),
            grid=(hk,),
            in_specs=[
                SMEM,
                block((rows, hd), lambda i: (0, i)),
                block((rows, hd), lambda i: (0, i)),
                block((None, hd, hd), lambda i: (i, 0, 0)),
            ],
            out_specs=[
                block((None, rows, feats), lambda i: (i, 0, 0)),
                block((None, count, tall, feats), lambda i: (i, 0, 0, 0)),
            ]
            + tail_specs,
            out_shape=[
                jax.ShapeDtypeStruct((hk, rows, feats), BF16),
                jax.ShapeDtypeStruct((hk, count, tall, feats), F32),
            ]
            + [rows_of((hi - lo) * tall, feats) for lo, hi in parts],
            compiler_params=pltpu.CompilerParams(vmem_limit_bytes=LIMIT),
            cost_estimate=cost(2 * hk * rows * hd * (hd + feats), hk * rows * hd * 4),
        )(doc_spans, k2, v2, k_map)
        feat_k, blocks, tails = out[0], out[1], out[2:]

        def exchange(own, reverse):
            came = []
            for k in range(hops):
                hop = 1 << k
                step = n_seq - hop if reverse else hop
                perm = [(i, (i + step) % n_seq) for i in range(n_seq)]
                got = lax.ppermute(own, "seq", perm)
                came.append(got)
                if k < hops - 1:
                    own = whole_call(
                        functools.partial(join_kernel, count, hop, reverse),
                        rows_of(*own.shape),
                        2,
                        own.size,
                        doc_spans,
                        own,
                        got,
                    )
            return came

        def middle(part, came):
            lo, hi = part
            state = block((tall, feats), lambda i, c: (i, 0))
            flops = 2 * (hi - lo) * group * rows * hd * (6 * feats + 3 * hd)
            grads = block((group * hd // 2, hd), lambda i, c: (i, 0))
            return pl.pallas_call(
                functools.partial(middle_kernel, count, group, hops, coef),
                grid=(hi - lo, count),
                in_specs=[
                    SMEM,
                    block((SPAN, group * hd), lambda i, c: (c, lo + i)),
                    block((SPAN, group * hd), lambda i, c: (c, lo + i)),
                    block((SPAN, hd), lambda i, c: (c, lo + i)),
                    block((None, SPAN, feats), lambda i, c: (lo + i, c, 0)),
                    block((group, hd, hd), lambda i, c: (lo + i, 0, 0)),
                    block((None, count, tall, feats), lambda i, c: (lo + i, 0, 0, 0)),
                ]
                + [state] * hops,
                out_specs=[
                    grads,
                    grads,
                    state,
                    block((None, None, tall, feats), lambda i, c: (i, c, 0, 0)),
                    block((None, None, SPAN, feats), lambda i, c: (i, c, 0, 0)),
                ],
                out_shape=[
                    rows_of((hi - lo) * group * hd // 2, hd),
                    rows_of((hi - lo) * group * hd // 2, hd),
                    rows_of((hi - lo) * tall, feats),
                    jax.ShapeDtypeStruct((hi - lo, count, tall, feats), F32),
                    jax.ShapeDtypeStruct((hi - lo, count, SPAN, feats), F32),
                ],
                compiler_params=pltpu.CompilerParams(vmem_limit_bytes=LIMIT),
                cost_estimate=cost(flops, 4 * rows * group * hd),
            )(doc_spans, q2, t2, v2, feat_k, q_map, blocks, *came)

        def last(part, back, inner, came):
            lo, hi = part
            return pl.pallas_call(
                functools.partial(last_kernel, count, hops),
                grid=(hi - lo,),
                in_specs=[
                    SMEM,
                    block((rows, hd), lambda i: (0, lo + i)),
                    block((rows, hd), lambda i: (0, lo + i)),
                    block((None, hd, hd), lambda i: (lo + i, 0, 0)),
                    block((None, count, tall, feats), lambda i: (i, 0, 0, 0)),
                    block((None, count, SPAN, feats), lambda i: (i, 0, 0, 0)),
                ]
                + [block((tall, feats), lambda i: (i, 0))] * hops,
                out_specs=block((hd, hd), lambda i: (i, 0)),
                out_shape=rows_of((hi - lo) * hd, hd),
                compiler_params=pltpu.CompilerParams(vmem_limit_bytes=LIMIT),
                cost_estimate=cost(LATE * rows * hd * 2 * feats, rows * feats * 4),
            )(doc_spans, k2, v2, k_map, back, inner, *came)

        total = Summer(n_dp, n_seq)
        came = [exchange(t, False) for t in tails]
        mids = [middle(p, c) for p, c in zip(parts, came)]
        halves, backs = [], []
        for mid in mids:
            keep, send = mid[0], mid[1]
            backs.append(exchange(mid[2], True))
            half_sum = total([[keep, total.send(send, total.core, 1)]], total.stages)
            halves += [half_sum, total.send(half_sum, total.core, 1)]
        gk = [last(p, m[3], m[4], b) for p, m, b in zip(parts, mids, backs)]
        grad_q = plain_call(
            functools.partial(assemble_kernel, parts, group * hd // 2), rows_of(hq * hd, hd), *halves
        )
        grad_k = total([[g] for g in gk], [total.core] + total.stages)
        return grad_q.reshape(hq, hd, hd), grad_k.reshape(hk, hd, hd)

    in_specs = (
        P("dp", "seq", None),
        P("dp", "seq", None),
        P("dp", "seq", None),
        P("dp", "seq", None),
        P(),
        P(),
        P("dp", None),
    )
    return jax.shard_map(
        shards, mesh=mesh, in_specs=in_specs, out_specs=(P(), P()), check_vma=False
    )
```

```python
import functools
import math

import jax
import jax.numpy as jnp
from jax import lax
from jax.experimental import pallas as pl
from jax.experimental.pallas import tpu as pltpu
from jax.sharding import PartitionSpec as P

SPAN = 128
PAD = 8
WHOLE = 128
F32 = jnp.float32
BF16 = jnp.bfloat16
NN = (((1,), (0,)), ((), ()))
NT = (((1,), (1,)), ((), ()))
TN = (((0,), (0,)), ((), ()))
TT = (((0,), (1,)), ((), ()))


def dot(left, right, dims):
    return lax.dot_general(left, right, dims, preferred_element_type=F32)


def bounds(spans_ref, block):
    start, end, place = jnp.int32(0), jnp.int32(0), jnp.int32(0)
    for d in range(spans_ref.shape[1]):
        after = place + spans_ref[0, d]
        inside = jnp.logical_and(block >= place, block < after)
        start = jnp.where(inside, place, start)
        end = jnp.where(inside, after, end)
        place = after
    return start, end


def flag(condition):
    return jnp.where(condition, jnp.float32(1.0), jnp.float32(0.0))


def soft_pair(mapped, axis):
    up = jnp.exp(mapped - jnp.max(mapped, axis, keepdims=True))
    low = jnp.exp(jnp.min(mapped, axis, keepdims=True) - mapped)
    up = up * (1.0 / jnp.sum(up, axis, keepdims=True))
    low = low * (1.0 / jnp.sum(low, axis, keepdims=True))
    return up, low


def map_grad(up, low, grad_up, grad_low, axis):
    first = up * (grad_up - jnp.sum(up * grad_up, axis, keepdims=True))
    second = low * (grad_low - jnp.sum(low * grad_low, axis, keepdims=True))
    return (first - second).astype(BF16)


def tall_rows(row):
    return jnp.broadcast_to(row, (PAD, row.shape[1]))


def key_kernel(count, parts, spans_ref, k_ref, v_ref, w_ref, feat_ref, block_ref, *tail_refs):
    width = w_ref.shape[-1]
    first = lax.axis_index("seq") * count
    starts = [bounds(spans_ref, first + c)[0] for c in range(count)]
    for (lo, hi), tail_ref in zip(parts, tail_refs):
        for i in range(lo, hi):
            cols = slice(i * width, (i + 1) * width)
            up, low = soft_pair(dot(k_ref[:, cols], w_ref[i], NN), -1)
            feat = jnp.concatenate([up, low], axis=-1).astype(BF16)
            feat_ref[i] = feat
            tail = None
            for c in range(count):
                rows = slice(c * SPAN, (c + 1) * SPAN)
                state = dot(v_ref[rows, cols], feat[rows], TN)
                norm = jnp.sum(feat[rows].astype(F32), axis=0, keepdims=True)
                both = jnp.concatenate([state, tall_rows(norm)], axis=0)
                block_ref[i, c] = both
                part = flag(starts[c] == starts[count - 1]) * both
                tail = part if tail is None else tail + part
            tall = tail.shape[0]
            tail_ref[(i - lo) * tall : (i - lo + 1) * tall] = tail


def join_kernel(count, hop, reverse, spans_ref, own_ref, came_ref, out_ref):
    place = lax.axis_index("seq")
    if reverse:
        _, end = bounds(spans_ref, place * count)
        keep = flag(end > (place + hop) * count)
    else:
        start, _ = bounds(spans_ref, place * count + count - 1)
        keep = flag(start < (place - hop + 1) * count)
    out_ref[...] = own_ref[...] + keep * came_ref[...]


def causal_mask(columns):
    t = lax.broadcasted_iota(jnp.int32, (SPAN, columns), 1) & (SPAN - 1)
    return lax.broadcasted_iota(jnp.int32, (SPAN, columns), 0) <= t


def early_kernel(part, count, group, *refs):
    q_ref, t_ref, v_ref, feat_k_ref, w_ref = refs[:5]
    up_ref, low_ref, feat_ref, num_ref, den_ref, tgt_ref = refs[5:]
    width = w_ref.shape[-1]
    causal = causal_mask(group * SPAN)
    for i in range(*part):
        k = i - part[0]
        for c in range(count):
            rows = slice(c * SPAN, (c + 1) * SPAN)
            cols = [slice(h * width, (h + 1) * width) for h in range(i * group, (i + 1) * group)]
            mapped = [dot(w_ref[i * group + h], q_ref[rows, cols[h]], TT) for h in range(group)]
            up, low = soft_pair(jnp.concatenate(mapped, axis=1), 0)
            up_ref[k, c] = up
            low_ref[k, c] = low
            feat = jnp.concatenate([up, low], axis=0).astype(BF16)
            feat_ref[k, c] = feat
            scores = jnp.where(causal, dot(feat_k_ref[i, rows], feat, NN), 0.0)
            den_ref[k, c] = tall_rows(jnp.sum(scores, 0, keepdims=True))
            vals = v_ref[rows, i * width : (i + 1) * width]
            num_ref[k, c] = dot(vals, scores.astype(BF16), TN)
            for h in range(group):
                tgt_ref[k, c, :, h * SPAN : (h + 1) * SPAN] = jnp.transpose(t_ref[rows, cols[h]])


def late_kernel(part, count, group, hops, coef, *refs):
    spans_ref, q_ref, v_ref, feat_k_ref, block_ref = refs[:5]
    up_ref, low_ref, feat_ref, num_ref, den_ref, tgt_ref = refs[5:11]
    came = refs[11 : 11 + hops]
    keep_ref, send_ref, head_ref, back_ref, inner_ref = refs[11 + hops :]
    width = tgt_ref.shape[2]
    tall = block_ref.shape[2]
    half = group // 2
    core = lax.axis_index("dp") & 1
    place = lax.axis_index("seq")
    first = place * count
    start_first, _ = bounds(spans_ref, first)
    causal = causal_mask(group * SPAN)
    for i in range(*part):
        k = i - part[0]
        grads, head = None, None
        for c in range(count):
            rows = slice(c * SPAN, (c + 1) * SPAN)
            start, _ = bounds(spans_ref, first + c)
            state = None
            for n in range(hops):
                near = start_first < (place - (1 << n) + 1) * count
                some = came[n][k * tall : (k + 1) * tall]
                some = flag(jnp.logical_and(near, start < first)) * some
                state = some if state is None else state + some
            for e in range(c):
                state = state + flag(start <= first + e) * block_ref[i, e]
            state = state.astype(BF16)
            feat_k = feat_k_ref[i, rows]
            feat = feat_ref[k, c]
            across = dot(state, feat, NN)
            numer = num_ref[k, c] + across[:SPAN]
            inverse = 1.0 / (den_ref[k, c, :1] + across[SPAN : SPAN + 1])
            output = numer * inverse
            d_out = coef * (output - tgt_ref[k, c].astype(F32))
            d_numer = (d_out * inverse).astype(BF16)
            d_denom = -jnp.sum(d_out * output, 0, keepdims=True) * inverse
            vals = v_ref[rows, i * width : (i + 1) * width]
            pairs = jnp.where(causal, dot(vals, d_numer, NN) + d_denom, 0.0).astype(BF16)
            mat = jnp.concatenate([feat_k, state[:SPAN]], axis=0)
            norm = jnp.transpose(state[SPAN:].astype(F32))[:, :1]
            d_feat = dot(mat, jnp.concatenate([pairs, d_numer], axis=0), TN) + norm * d_denom
            high = d_denom.astype(BF16)
            rest = d_denom - high.astype(F32)
            mid = rest.astype(BF16)
            low = (rest - mid.astype(F32)).astype(BF16)
            fill = jnp.zeros((2 * PAD - 3, high.shape[1]), BF16)
            left = jnp.concatenate([d_numer, pairs, high, mid, low, fill], axis=0)
            crossed = dot(left, feat, NT)
            at = 2 * SPAN
            norm_row = crossed[at : at + 1] + crossed[at + 1 : at + 2] + crossed[at + 2 : at + 3]
            back = jnp.concatenate([crossed[:SPAN], tall_rows(norm_row)], axis=0)
            back_ref[k, c] = back
            inner_ref[k, c] = crossed[SPAN:at]
            d_map = map_grad(up_ref[k, c], low_ref[k, c], d_feat[:width], d_feat[width:], 0)
            now = []
            for h in range(group):
                queries = q_ref[rows, (i * group + h) * width : (i * group + h + 1) * width]
                now.append(dot(d_map[:, h * SPAN : (h + 1) * SPAN], queries, NN))
            grads = now if grads is None else [a + b for a, b in zip(grads, now)]
            mine = flag(start == start_first) * back
            head = mine if head is None else head + mine
        head_ref[k * tall : (k + 1) * tall] = head
        for h in range(half):
            at = slice((k * half + h) * width, (k * half + h + 1) * width)
            keep_ref[at] = jnp.transpose(jnp.where(core == 0, grads[h], grads[half + h]))
            send_ref[at] = jnp.transpose(jnp.where(core == 0, grads[half + h], grads[h]))


def last_kernel(part, count, hops, *refs):
    spans_ref, k_ref, v_ref, w_ref, back_ref, inner_ref = refs[:6]
    came = refs[6 : 6 + hops]
    gk_ref = refs[6 + hops]
    width = w_ref.shape[-1]
    tall = back_ref.shape[2]
    place = lax.axis_index("seq")
    first = place * count
    _, end_last = bounds(spans_ref, first + count - 1)
    for i in range(*part):
        k = i - part[0]
        cols = slice(i * width, (i + 1) * width)
        keys = k_ref[:, cols]
        up, low = soft_pair(dot(keys, w_ref[i], NN), -1)
        grads = []
        for c in range(count):
            _, end = bounds(spans_ref, first + c)
            state = None
            for n in range(hops):
                near = end_last > (place + (1 << n)) * count
                some = came[n][k * tall : (k + 1) * tall]
                some = flag(jnp.logical_and(near, end > first + count)) * some
                state = some if state is None else state + some
            for e in range(c + 1, count):
                state = state + flag(end > first + e) * back_ref[k, e]
            norm = state[SPAN : SPAN + 1].astype(BF16).astype(F32)
            vals = v_ref[c * SPAN : (c + 1) * SPAN, cols]
            grads.append(inner_ref[k, c] + dot(vals, state[:SPAN].astype(BF16), NN) + norm)
        d_feat = jnp.concatenate(grads, axis=0)
        d_map = map_grad(up, low, d_feat[:, :width], d_feat[:, width:], -1)
        gk_ref[k * width : (k + 1) * width] = dot(keys, d_map, TN)


def cost(flops, moved):
    return pl.CostEstimate(flops=int(flops), bytes_accessed=int(moved), transcendentals=0)


SMEM = pl.BlockSpec(memory_space=pltpu.SMEM)
LIMIT = 32 << 20
PER_MICRO = 1e9


def local_call(body, out_shape, micros, *args, spans=None):
    first = [] if spans is None else [spans]
    return pl.pallas_call(
        body,
        out_shape=out_shape,
        in_specs=[SMEM] * len(first) + [pl.BlockSpec(memory_space=pltpu.VMEM)] * len(args),
        compiler_params=pltpu.CompilerParams(vmem_limit_bytes=LIMIT),
        cost_estimate=cost(micros * PER_MICRO, 0),
    )(*first, *args)


def index_in(stage):
    place = jnp.int32(0)
    for k, (axis, bit) in enumerate(stage):
        place = place + (((lax.axis_index(axis) >> bit) & 1) << k)
    return place


def split_kernel(stage, layout, *refs):
    pieces = 1 << len(stage)
    outs = refs[len(refs) - pieces :]
    mine = index_in(stage)
    for m, out in enumerate(outs):
        at, used = 0, 0
        for addends, rows in layout:
            size = rows // pieces
            start = 0 if pieces == 1 else pl.multiple_of((mine ^ m) * size, PAD)
            total = refs[used][pl.ds(start, size), :]
            for ref in refs[used + 1 : used + addends]:
                total = total + ref[pl.ds(start, size), :]
            out[at : at + size] = total
            at, used = at + size, used + addends


def join_pieces_kernel(stage, layout, *refs):
    pieces = 1 << len(stage)
    out = refs[pieces]
    mine = index_in(stage)
    for m in range(pieces):
        at, base = 0, 0
        for _, rows in layout:
            size = rows // pieces
            start = pl.multiple_of(base + (mine ^ m) * size, PAD)
            out[pl.ds(start, size), :] = refs[m][at : at + size]
            at, base = at + size, base + rows


def pack_kernel(stage, cut, x_ref, extra_ref, *outs):
    own = x_ref.shape[0]
    mine = index_in(stage)
    size = extra_ref.shape[0] // (len(outs) if cut else 1)
    for m, out in enumerate(outs):
        start = pl.multiple_of((mine ^ m) * size, PAD) if cut else 0
        out[:own] = x_ref[...]
        out[own:] = extra_ref[pl.ds(start, size), :]


def merge_kernel(stage, layout, *refs):
    pieces = 1 << len(stage)
    join_pieces_kernel(stage, layout, *refs[: pieces + 1])
    own = sum(rows for _, rows in layout) // pieces
    total = refs[0][own:]
    for ref in refs[1:pieces]:
        total = total + ref[own:]
    refs[pieces + 1][...] = total


def rows_of(rows, width):
    return jax.ShapeDtypeStruct((rows, width), F32)


class Summer:
    def __init__(self, n_dp, n_seq):
        self.n_dp, self.n_seq = n_dp, n_seq
        bits = [("dp", b) for b in range(1, n_dp.bit_length() - 1)]
        seq = [("seq", b) for b in range(n_seq.bit_length() - 1)]
        rest = bits[:1] + seq[:1] + seq[1:] + bits[1:]
        self.core = [("dp", 0)]
        self.stages = [rest[k : k + 2] for k in range(0, len(rest), 2)]

    def send(self, x, stage, mask):
        d_mask = sum(1 << b for k, (a, b) in enumerate(stage) if a == "dp" and mask >> k & 1)
        s_mask = sum(1 << b for k, (a, b) in enumerate(stage) if a == "seq" and mask >> k & 1)
        perm = [
            (d * self.n_seq + s, (d ^ d_mask) * self.n_seq + (s ^ s_mask))
            for d in range(self.n_dp)
            for s in range(self.n_seq)
        ]
        return lax.ppermute(x, ("dp", "seq"), perm)

    def split(self, groups, stage):
        pieces = 1 << len(stage)
        layout = [(len(g), g[0].shape[0]) for g in groups]
        size = sum(rows for _, rows in layout) // pieces
        width = groups[0][0].shape[1]
        out = local_call(
            functools.partial(split_kernel, stage, layout),
            [rows_of(size, width)] * pieces,
            0.4,
            *[a for g in groups for a in g],
        )
        return out, layout

    def join(self, x, stage, layout):
        came = [x] + [self.send(x, stage, m) for m in range(1, 1 << len(stage))]
        total = sum(rows for _, rows in layout)
        return local_call(
            functools.partial(join_pieces_kernel, stage, layout),
            rows_of(total, x.shape[1]),
            0.4,
            *came,
        )

    def scatter(self, groups, stage):
        rows = [g[0].shape[0] for g in groups]
        if sum(rows) > WHOLE and min(rows) >> len(stage) >= PAD:
            out, layout = self.split(groups, stage)
        else:
            whole, layout = self.split(groups, [])
            out, layout = [whole[0]] * (1 << len(stage)), None
        return [[out[0]] + [self.send(out[m], stage, m) for m in range(1, len(out))]], layout

    def gather(self, x, stage, layout):
        return x if layout is None else self.join(x, stage, layout)

    def gather_with(self, x, stage, layout, extra, last_stage):
        if layout is None:
            groups, extra_layout = self.scatter([[extra]], stage)
            return x, self.split(groups, [])[0][0], extra_layout
        pieces = 1 << len(stage)
        rows, width = extra.shape
        cut = not last_stage and rows // pieces >= PAD
        size = rows // pieces if cut else rows
        own = x.shape[0]
        out = local_call(
            functools.partial(pack_kernel, stage, cut),
            [rows_of(own + size, width)] * (pieces if cut else 1),
            0.4,
            x,
            extra,
        )
        out = out if cut else out * pieces
        came = [out[0]] + [self.send(out[m], stage, m) for m in range(1, pieces)]
        total = sum(r for _, r in layout)
        x, extra = local_call(
            functools.partial(merge_kernel, stage, layout),
            [rows_of(total, width), rows_of(size, width)],
            0.4,
            *came,
        )
        return x, extra, [(1, rows)] if cut else None


def assemble_kernel(heads, half, own_ref, came_ref, out_ref):
    mine = lax.axis_index("dp") & 1
    for side, ref in enumerate((own_ref, came_ref)):
        for i in range(heads):
            start = pl.multiple_of((2 * i + (mine ^ side)) * half, PAD)
            out_ref[pl.ds(start, half), :] = ref[i * half : (i + 1) * half]


def solution(mesh):
    n_dp, n_seq = mesh.shape["dp"], mesh.shape["seq"]

    def shards(queries, keys, values, targets, q_map, k_map, doc_spans):
        hq, hd = q_map.shape[0], q_map.shape[1]
        hk = k_map.shape[0]
        group = hq // hk
        rows = queries.shape[1]
        count = rows // SPAN
        feats = 2 * hd
        tall = SPAN + PAD
        coef = 2.0 / math.sqrt(n_dp * n_seq * rows * hd)
        most = (3 * n_seq * count) // 8
        before = min(n_seq - 1, -(-(most - 1) // count))
        hops = max(1, before.bit_length())
        q2, t2 = queries[0], targets[0]
        k2, v2 = keys[0], values[0]
        parts = [(0, hk // 2), (hk // 2, hk)]
        array = jax.ShapeDtypeStruct
        out = local_call(
            functools.partial(key_kernel, count, parts),
            [array((hk, rows, feats), BF16), array((hk, count, tall, feats), F32)]
            + [rows_of((hi - lo) * tall, feats) for lo, hi in parts],
            3.0,
            k2,
            v2,
            k_map,
            spans=doc_spans,
        )
        feat_k, blocks, tails = out[0], out[1], out[2:]

        def shift(own, hop, reverse):
            step = n_seq - hop if reverse else hop
            return lax.ppermute(own, "seq", [(i, (i + step) % n_seq) for i in range(n_seq)])

        def join(own, got, hop, reverse):
            return local_call(
                functools.partial(join_kernel, count, hop, reverse),
                rows_of(*own.shape),
                0.6,
                own,
                got,
                spans=doc_spans,
            )

        def exchange(own, reverse, start=0):
            came = []
            for k in range(start, hops):
                came.append(shift(own, 1 << k, reverse))
                if k < hops - 1:
                    own = join(own, came[-1], 1 << k, reverse)
            return came

        def early(part):
            wide = lambda r, dtype: array((part[1] - part[0], count, r, group * SPAN), dtype)
            return local_call(
                functools.partial(early_kernel, part, count, group),
                [wide(hd, F32), wide(hd, F32), wide(feats, BF16), wide(hd, F32), wide(PAD, F32)]
                + [wide(hd, BF16)],
                3.0,
                q2,
                t2,
                v2,
                feat_k,
                q_map,
            )

        def late(part, ready, came):
            heads = part[1] - part[0]
            return local_call(
                functools.partial(late_kernel, part, count, group, hops, coef),
                [rows_of(heads * group * hd // 2, hd)] * 2
                + [rows_of(heads * tall, feats)]
                + [array((heads, count, tall, feats), F32), array((heads, count, SPAN, feats), F32)],
                6.0,
                q2,
                v2,
                feat_k,
                blocks,
                *ready,
                *came,
                spans=doc_spans,
            )

        def last(part, back, inner, came):
            return local_call(
                functools.partial(last_kernel, part, count, hops),
                rows_of((part[1] - part[0]) * hd, hd),
                1.5,
                k2,
                v2,
                k_map,
                back,
                inner,
                *came,
                spans=doc_spans,
            )

        total = Summer(n_dp, n_seq)
        came = [exchange(t, False) for t in tails]
        ready = [early(p) for p in parts]
        first = late(parts[0], ready[0], came[0])
        back_one = shift(first[2], 1, True)
        core_one = total.send(first[1], total.core, 1)
        second = late(parts[1], ready[1], came[1])
        joined = join(first[2], back_one, 1, True)
        joined, core_one, *second = lax.optimization_barrier((joined, core_one, *second))
        back_two = [shift(second[2], 1, True)]
        core_two = total.send(second[1], total.core, 1)
        back_one = [back_one] + exchange(joined, True, 1)
        groups, layout = total.scatter([[first[0], core_one], [second[0], core_two]], total.stages[0])
        layouts = [layout]
        joined = join(second[2], back_two[0], 1, True)
        groups, joined, back_one = lax.optimization_barrier((groups, joined, back_one))
        back_two += exchange(joined, True, 1)
        for stage in total.stages[1:]:
            groups, layout = total.scatter(groups, stage)
            layouts.append(layout)
        x = total.split(groups, [])[0][0]
        x, back_two = lax.optimization_barrier((x, back_two))
        gk = [
            last(p, m[3], m[4], b)
            for p, m, b in zip(parts, (first, second), (back_one, back_two))
        ]
        out, core_layout = total.split([[g] for g in gk], total.core)
        extra = total.split([[out[0], total.send(out[1], total.core, 1)]], [])[0][0]
        x, extra = lax.optimization_barrier((x, extra))
        extra_layouts = []
        for k in reversed(range(len(total.stages))):
            x, extra, layout = total.gather_with(x, total.stages[k], layouts[k], extra, k == 0)
            extra_layouts.append((total.stages[k], layout))
        halves = [x, total.send(x, total.core, 1)]
        for stage, layout in reversed(extra_layouts):
            extra = total.gather(extra, stage, layout)
        grad_q = local_call(
            functools.partial(assemble_kernel, hk, group * hd // 2),
            rows_of(hq * hd, hd),
            1.0,
            *halves,
        )
        grad_k = total.join(extra, total.core, core_layout)
        return grad_q.reshape(hq, hd, hd), grad_k.reshape(hk, hd, hd)

    in_specs = (
        P("dp", "seq", None),
        P("dp", "seq", None),
        P("dp", "seq", None),
        P("dp", "seq", None),
        P(),
        P(),
        P("dp", None),
    )
    return jax.shard_map(
        shards, mesh=mesh, in_specs=in_specs, out_specs=(P(), P()), check_vma=False
    )
```

```python
import functools
import math

import jax
import jax.numpy as jnp
from jax import lax
from jax.experimental import pallas as pl
from jax.experimental.pallas import tpu as pltpu
from jax.sharding import PartitionSpec as P

SPAN = 128
PAD = 8
WHOLE = 128
F32 = jnp.float32
BF16 = jnp.bfloat16
NN = (((1,), (0,)), ((), ()))
NT = (((1,), (1,)), ((), ()))
TN = (((0,), (0,)), ((), ()))
TT = (((0,), (1,)), ((), ()))


def dot(left, right, dims):
    return lax.dot_general(left, right, dims, preferred_element_type=F32)


def bounds(spans_ref, block):
    start, end, place = jnp.int32(0), jnp.int32(0), jnp.int32(0)
    for d in range(spans_ref.shape[1]):
        after = place + spans_ref[0, d]
        inside = jnp.logical_and(block >= place, block < after)
        start = jnp.where(inside, place, start)
        end = jnp.where(inside, after, end)
        place = after
    return start, end


def flag(condition):
    return jnp.where(condition, jnp.float32(1.0), jnp.float32(0.0))


def soft_pair(mapped, axis):
    up = jnp.exp(mapped - jnp.max(mapped, axis, keepdims=True))
    low = jnp.exp(jnp.min(mapped, axis, keepdims=True) - mapped)
    up = up * (1.0 / jnp.sum(up, axis, keepdims=True))
    low = low * (1.0 / jnp.sum(low, axis, keepdims=True))
    return up, low


def map_grad(up, low, grad_up, grad_low, axis):
    first = up * (grad_up - jnp.sum(up * grad_up, axis, keepdims=True))
    second = low * (grad_low - jnp.sum(low * grad_low, axis, keepdims=True))
    return (first - second).astype(BF16)


def tall_rows(row):
    return jnp.broadcast_to(row, (PAD, row.shape[1]))


def key_kernel(count, parts, spans_hbm, k_hbm, v_hbm, w_hbm, feat_ref, block_ref, *rest):
    tail_refs = rest[: len(parts)]
    spans_ref, k_ref, v_ref, w_ref, sems = rest[len(parts) :]
    pairs = [(spans_hbm, spans_ref), (k_hbm, k_ref), (w_hbm, w_ref), (v_hbm, v_ref)]
    copies = [pltpu.make_async_copy(a, b, sems.at[n]) for n, (a, b) in enumerate(pairs)]
    for copy in copies:
        copy.start()
    for copy in copies:
        copy.wait()
    width = w_ref.shape[-1]
    first = lax.axis_index("seq") * count
    starts = [bounds(spans_ref, first + c)[0] for c in range(count)]
    for (lo, hi), tail_ref in zip(parts, tail_refs):
        for i in range(lo, hi):
            cols = slice(i * width, (i + 1) * width)
            up, low = soft_pair(dot(k_ref[:, cols], w_ref[i], NN), -1)
            feat = jnp.concatenate([up, low], axis=-1).astype(BF16)
            feat_ref[i] = feat
            tail = None
            for c in range(count):
                rows = slice(c * SPAN, (c + 1) * SPAN)
                state = dot(v_ref[rows, cols], feat[rows], TN)
                norm = jnp.sum(feat[rows].astype(F32), axis=0, keepdims=True)
                both = jnp.concatenate([state, tall_rows(norm)], axis=0)
                block_ref[i, c] = both
                part = flag(starts[c] == starts[count - 1]) * both
                tail = part if tail is None else tail + part
            tall = tail.shape[0]
            tail_ref[(i - lo) * tall : (i - lo + 1) * tall] = tail


def join_kernel(count, hop, reverse, spans_ref, own_ref, came_ref, out_ref):
    place = lax.axis_index("seq")
    if reverse:
        _, end = bounds(spans_ref, place * count)
        keep = flag(end > (place + hop) * count)
    else:
        start, _ = bounds(spans_ref, place * count + count - 1)
        keep = flag(start < (place - hop + 1) * count)
    out_ref[...] = own_ref[...] + keep * came_ref[...]


def causal_mask(columns):
    t = lax.broadcasted_iota(jnp.int32, (SPAN, columns), 1) & (SPAN - 1)
    return lax.broadcasted_iota(jnp.int32, (SPAN, columns), 0) <= t


def early_kernel(part, count, group, *refs):
    q_ref, t_ref, v_ref, feat_k_ref, w_ref = refs[:5]
    up_ref, low_ref, feat_ref, num_ref, den_ref, tgt_ref = refs[5:]
    width = w_ref.shape[-1]
    causal = causal_mask(group * SPAN)
    for i in range(*part):
        k = i - part[0]
        for c in range(count):
            rows = slice(c * SPAN, (c + 1) * SPAN)
            cols = [slice(h * width, (h + 1) * width) for h in range(i * group, (i + 1) * group)]
            mapped = [dot(w_ref[i * group + h], q_ref[rows, cols[h]], TT) for h in range(group)]
            up, low = soft_pair(jnp.concatenate(mapped, axis=1), 0)
            up_ref[k, c] = up
            low_ref[k, c] = low
            feat = jnp.concatenate([up, low], axis=0).astype(BF16)
            feat_ref[k, c] = feat
            scores = jnp.where(causal, dot(feat_k_ref[i, rows], feat, NN), 0.0)
            den_ref[k, c] = tall_rows(jnp.sum(scores, 0, keepdims=True))
            vals = v_ref[rows, i * width : (i + 1) * width]
            num_ref[k, c] = dot(vals, scores.astype(BF16), TN)
            for h in range(group):
                tgt_ref[k, c, :, h * SPAN : (h + 1) * SPAN] = jnp.transpose(t_ref[rows, cols[h]])


def late_kernel(part, count, group, hops, coef, *refs):
    spans_ref, q_ref, v_ref, feat_k_ref, block_ref = refs[:5]
    up_ref, low_ref, feat_ref, num_ref, den_ref, tgt_ref = refs[5:11]
    came = refs[11 : 11 + hops]
    keep_ref, send_ref, head_ref, back_ref, inner_ref = refs[11 + hops :]
    width = tgt_ref.shape[2]
    tall = block_ref.shape[2]
    half = group // 2
    core = lax.axis_index("dp") & 1
    place = lax.axis_index("seq")
    first = place * count
    start_first, _ = bounds(spans_ref, first)
    causal = causal_mask(group * SPAN)
    for i in range(*part):
        k = i - part[0]
        grads, head = None, None
        for c in range(count):
            rows = slice(c * SPAN, (c + 1) * SPAN)
            start, _ = bounds(spans_ref, first + c)
            state = None
            for n in range(hops):
                near = start_first < (place - (1 << n) + 1) * count
                some = came[n][k * tall : (k + 1) * tall]
                some = flag(jnp.logical_and(near, start < first)) * some
                state = some if state is None else state + some
            for e in range(c):
                state = state + flag(start <= first + e) * block_ref[i, e]
            state = state.astype(BF16)
            feat_k = feat_k_ref[i, rows]
            feat = feat_ref[k, c]
            across = dot(state, feat, NN)
            numer = num_ref[k, c] + across[:SPAN]
            inverse = 1.0 / (den_ref[k, c, :1] + across[SPAN : SPAN + 1])
            output = numer * inverse
            d_out = coef * (output - tgt_ref[k, c].astype(F32))
            d_numer = (d_out * inverse).astype(BF16)
            d_denom = -jnp.sum(d_out * output, 0, keepdims=True) * inverse
            vals = v_ref[rows, i * width : (i + 1) * width]
            pairs = jnp.where(causal, dot(vals, d_numer, NN) + d_denom, 0.0).astype(BF16)
            mat = jnp.concatenate([feat_k, state[:SPAN]], axis=0)
            norm = jnp.transpose(state[SPAN:].astype(F32))[:, :1]
            d_feat = dot(mat, jnp.concatenate([pairs, d_numer], axis=0), TN) + norm * d_denom
            high = d_denom.astype(BF16)
            rest = d_denom - high.astype(F32)
            mid = rest.astype(BF16)
            low = (rest - mid.astype(F32)).astype(BF16)
            fill = jnp.zeros((2 * PAD - 3, high.shape[1]), BF16)
            left = jnp.concatenate([d_numer, pairs, high, mid, low, fill], axis=0)
            crossed = dot(left, feat, NT)
            at = 2 * SPAN
            norm_row = crossed[at : at + 1] + crossed[at + 1 : at + 2] + crossed[at + 2 : at + 3]
            back = jnp.concatenate([crossed[:SPAN], tall_rows(norm_row)], axis=0)
            back_ref[k, c] = back
            inner_ref[k, c] = crossed[SPAN:at]
            d_map = map_grad(up_ref[k, c], low_ref[k, c], d_feat[:width], d_feat[width:], 0)
            now = []
            for h in range(group):
                queries = q_ref[rows, (i * group + h) * width : (i * group + h + 1) * width]
                now.append(dot(d_map[:, h * SPAN : (h + 1) * SPAN], queries, NN))
            grads = now if grads is None else [a + b for a, b in zip(grads, now)]
            mine = flag(start == start_first) * back
            head = mine if head is None else head + mine
        head_ref[k * tall : (k + 1) * tall] = head
        for h in range(half):
            at = slice((k * half + h) * width, (k * half + h + 1) * width)
            keep_ref[at] = jnp.transpose(jnp.where(core == 0, grads[h], grads[half + h]))
            send_ref[at] = jnp.transpose(jnp.where(core == 0, grads[half + h], grads[h]))


def last_kernel(part, count, hops, *refs):
    spans_ref, k_ref, v_ref, w_ref, back_ref, inner_ref = refs[:6]
    came = refs[6 : 6 + hops]
    gk_ref = refs[6 + hops]
    width = w_ref.shape[-1]
    tall = back_ref.shape[2]
    place = lax.axis_index("seq")
    first = place * count
    _, end_last = bounds(spans_ref, first + count - 1)
    for i in range(*part):
        k = i - part[0]
        cols = slice(i * width, (i + 1) * width)
        keys = k_ref[:, cols]
        up, low = soft_pair(dot(keys, w_ref[i], NN), -1)
        grads = []
        for c in range(count):
            _, end = bounds(spans_ref, first + c)
            state = None
            for n in range(hops):
                near = end_last > (place + (1 << n)) * count
                some = came[n][k * tall : (k + 1) * tall]
                some = flag(jnp.logical_and(near, end > first + count)) * some
                state = some if state is None else state + some
            for e in range(c + 1, count):
                state = state + flag(end > first + e) * back_ref[k, e]
            norm = state[SPAN : SPAN + 1].astype(BF16).astype(F32)
            vals = v_ref[c * SPAN : (c + 1) * SPAN, cols]
            grads.append(inner_ref[k, c] + dot(vals, state[:SPAN].astype(BF16), NN) + norm)
        d_feat = jnp.concatenate(grads, axis=0)
        d_map = map_grad(up, low, d_feat[:, :width], d_feat[:, width:], -1)
        gk_ref[k * width : (k + 1) * width] = dot(keys, d_map, TN)


def cost(flops, moved):
    return pl.CostEstimate(flops=int(flops), bytes_accessed=int(moved), transcendentals=0)


SMEM = pl.BlockSpec(memory_space=pltpu.SMEM)
LIMIT = 32 << 20
PER_MICRO = 1e9


def local_call(body, out_shape, micros, *args, spans=None):
    first = [] if spans is None else [spans]
    return pl.pallas_call(
        body,
        out_shape=out_shape,
        in_specs=[SMEM] * len(first) + [pl.BlockSpec(memory_space=pltpu.VMEM)] * len(args),
        compiler_params=pltpu.CompilerParams(vmem_limit_bytes=LIMIT),
        cost_estimate=cost(micros * PER_MICRO, 0),
    )(*first, *args)


def index_in(stage):
    place = jnp.int32(0)
    for k, (axis, bit) in enumerate(stage):
        place = place + (((lax.axis_index(axis) >> bit) & 1) << k)
    return place


def split_kernel(stage, layout, *refs):
    pieces = 1 << len(stage)
    outs = refs[len(refs) - pieces :]
    mine = index_in(stage)
    for m, out in enumerate(outs):
        at, used = 0, 0
        for addends, rows in layout:
            size = rows // pieces
            start = 0 if pieces == 1 else pl.multiple_of((mine ^ m) * size, PAD)
            total = refs[used][pl.ds(start, size), :]
            for ref in refs[used + 1 : used + addends]:
                total = total + ref[pl.ds(start, size), :]
            out[at : at + size] = total
            at, used = at + size, used + addends


def join_pieces_kernel(stage, layout, *refs):
    pieces = 1 << len(stage)
    out = refs[pieces]
    mine = index_in(stage)
    for m in range(pieces):
        at, base = 0, 0
        for _, rows in layout:
            size = rows // pieces
            start = pl.multiple_of(base + (mine ^ m) * size, PAD)
            out[pl.ds(start, size), :] = refs[m][at : at + size]
            at, base = at + size, base + rows


def rows_of(rows, width):
    return jax.ShapeDtypeStruct((rows, width), F32)


class Summer:
    def __init__(self, n_dp, n_seq):
        self.n_dp, self.n_seq = n_dp, n_seq
        bits = [("dp", b) for b in range(1, n_dp.bit_length() - 1)]
        seq = [("seq", b) for b in range(n_seq.bit_length() - 1)]
        rest = bits[:1] + seq[:1] + seq[1:] + bits[1:]
        self.core = [("dp", 0)]
        self.stages = [rest[k : k + 2] for k in range(0, len(rest), 2)]

    def send(self, x, stage, mask):
        d_mask = sum(1 << b for k, (a, b) in enumerate(stage) if a == "dp" and mask >> k & 1)
        s_mask = sum(1 << b for k, (a, b) in enumerate(stage) if a == "seq" and mask >> k & 1)
        perm = [
            (d * self.n_seq + s, (d ^ d_mask) * self.n_seq + (s ^ s_mask))
            for d in range(self.n_dp)
            for s in range(self.n_seq)
        ]
        return lax.ppermute(x, ("dp", "seq"), perm)

    def split(self, groups, stage):
        pieces = 1 << len(stage)
        layout = [(len(g), g[0].shape[0]) for g in groups]
        size = sum(rows for _, rows in layout) // pieces
        width = groups[0][0].shape[1]
        out = local_call(
            functools.partial(split_kernel, stage, layout),
            [rows_of(size, width)] * pieces,
            0.4,
            *[a for g in groups for a in g],
        )
        return out, layout

    def join(self, x, stage, layout):
        came = [x] + [self.send(x, stage, m) for m in range(1, 1 << len(stage))]
        total = sum(rows for _, rows in layout)
        return local_call(
            functools.partial(join_pieces_kernel, stage, layout),
            rows_of(total, x.shape[1]),
            0.4,
            *came,
        )

    def scatter(self, groups, stage, whole=WHOLE):
        rows = [g[0].shape[0] for g in groups]
        if sum(rows) > whole and min(rows) >> len(stage) >= PAD:
            out, layout = self.split(groups, stage)
        else:
            whole, layout = self.split(groups, [])
            out, layout = [whole[0]] * (1 << len(stage)), None
        return [[out[0]] + [self.send(out[m], stage, m) for m in range(1, len(out))]], layout

    def gather(self, x, stage, layout):
        return x if layout is None else self.join(x, stage, layout)


def assemble_kernel(heads, half, own_ref, came_ref, out_ref):
    mine = lax.axis_index("dp") & 1
    for side, ref in enumerate((own_ref, came_ref)):
        for i in range(heads):
            start = pl.multiple_of((2 * i + (mine ^ side)) * half, PAD)
            out_ref[pl.ds(start, half), :] = ref[i * half : (i + 1) * half]


def solution(mesh):
    n_dp, n_seq = mesh.shape["dp"], mesh.shape["seq"]

    def shards(queries, keys, values, targets, q_map, k_map, doc_spans):
        hq, hd = q_map.shape[0], q_map.shape[1]
        hk = k_map.shape[0]
        group = hq // hk
        rows = queries.shape[1]
        count = rows // SPAN
        feats = 2 * hd
        tall = SPAN + PAD
        coef = 2.0 / math.sqrt(n_dp * n_seq * rows * hd)
        most = (3 * n_seq * count) // 8
        before = min(n_seq - 1, -(-(most - 1) // count))
        hops = max(1, before.bit_length())
        q2, t2 = queries[0], targets[0]
        k2, v2 = keys[0], values[0]
        parts = [(0, hk // 2), (hk // 2, hk)]
        array = jax.ShapeDtypeStruct
        out = pl.pallas_call(
            functools.partial(key_kernel, count, parts),
            out_shape=[array((hk, rows, feats), BF16), array((hk, count, tall, feats), F32)]
            + [rows_of((hi - lo) * tall, feats) for lo, hi in parts],
            in_specs=[pl.BlockSpec(memory_space=pl.ANY)] * 4,
            scratch_shapes=[
                pltpu.SMEM(doc_spans.shape, jnp.int32),
                pltpu.VMEM(k2.shape, BF16),
                pltpu.VMEM(v2.shape, BF16),
                pltpu.VMEM(k_map.shape, BF16),
                pltpu.SemaphoreType.DMA((4,)),
            ],
            compiler_params=pltpu.CompilerParams(vmem_limit_bytes=LIMIT),
            cost_estimate=cost(3 * PER_MICRO, 0),
        )(doc_spans, k2, v2, k_map)
        feat_k, blocks, tails = out[0], out[1], out[2:]

        def shift(own, hop, reverse):
            step = -hop if reverse else hop
            ring = [(i, (i + step) % n_seq) for i in range(n_seq)]
            return lax.ppermute(own, "seq", ring)

        def join(own, got, hop, reverse):
            return local_call(
                functools.partial(join_kernel, count, hop, reverse),
                rows_of(*own.shape),
                0.6,
                own,
                got,
                spans=doc_spans,
            )

        def exchange(own, reverse, start=0):
            came = []
            for k in range(start, hops):
                came.append(shift(own, 1 << k, reverse))
                if k < hops - 1:
                    own = join(own, came[-1], 1 << k, reverse)
            return came

        def early(part):
            wide = lambda r, dtype: array((part[1] - part[0], count, r, group * SPAN), dtype)
            return local_call(
                functools.partial(early_kernel, part, count, group),
                [wide(hd, F32), wide(hd, F32), wide(feats, BF16), wide(hd, F32), wide(PAD, F32)]
                + [wide(hd, BF16)],
                3.0,
                q2,
                t2,
                v2,
                feat_k,
                q_map,
            )

        def late(part, ready, came):
            heads = part[1] - part[0]
            return local_call(
                functools.partial(late_kernel, part, count, group, hops, coef),
                [rows_of(heads * group * hd // 2, hd)] * 2
                + [rows_of(heads * tall, feats)]
                + [array((heads, count, tall, feats), F32), array((heads, count, SPAN, feats), F32)],
                6.0,
                q2,
                v2,
                feat_k,
                blocks,
                *ready,
                *came,
                spans=doc_spans,
            )

        def last(part, back, inner, came):
            return local_call(
                functools.partial(last_kernel, part, count, hops),
                rows_of((part[1] - part[0]) * hd, hd),
                1.5,
                k2,
                v2,
                k_map,
                back,
                inner,
                *came,
                spans=doc_spans,
            )

        total = Summer(n_dp, n_seq)
        came = [exchange(t, False) for t in tails]
        ready = [early(p) for p in parts]
        first = late(parts[0], ready[0], came[0])
        back_one = shift(first[2], 1, True)
        core_one = total.send(first[1], total.core, 1)
        second = late(parts[1], ready[1], came[1])
        core_one, back_one, *second = lax.optimization_barrier((core_one, back_one, *second))
        back_two = [shift(second[2], 1, True)]
        core_two = total.send(second[1], total.core, 1)
        joined = join(first[2], back_one, 1, True)
        joined, core_two = lax.optimization_barrier((joined, core_two))
        back_one = [back_one] + exchange(joined, True, 1)
        groups, layout = total.scatter([[first[0], core_one], [second[0], core_two]], total.stages[0])
        layouts = [layout]
        joined = join(second[2], back_two[0], 1, True)
        groups, joined, back_one = lax.optimization_barrier((groups, joined, back_one))
        back_two += exchange(joined, True, 1)
        for stage in total.stages[1:]:
            groups, layout = total.scatter(groups, stage)
            layouts.append(layout)
        x = total.split(groups, [])[0][0]
        x, back_two = lax.optimization_barrier((x, back_two))
        for stage, layout in reversed(list(zip(total.stages[1:], layouts[1:]))):
            x = total.gather(x, stage, layout)
        gk = [
            last(p, m[3], m[4], b)
            for p, m, b in zip(parts, (first, second), (back_one, back_two))
        ]
        out, core_layout = total.split([[g] for g in gk], total.core)
        extra = [[out[0], total.send(out[1], total.core, 1)]]
        extra, layout = total.scatter(extra, total.stages[0], 2 * WHOLE)
        extra_layouts = [layout]
        x, extra = lax.optimization_barrier((x, extra))
        x = total.gather(x, total.stages[0], layouts[0])
        for stage in total.stages[1:]:
            extra, layout = total.scatter(extra, stage, 2 * WHOLE)
            extra_layouts.append(layout)
        extra = total.split(extra, [])[0][0]
        for stage, layout in reversed(list(zip(total.stages, extra_layouts))):
            extra = total.gather(extra, stage, layout)
        x, extra = lax.optimization_barrier((x, extra))
        halves = [x, total.send(x, total.core, 1)]
        grad_q = local_call(
            functools.partial(assemble_kernel, hk, group * hd // 2),
            rows_of(hq * hd, hd),
            1.0,
            *halves,
        )
        grad_k = total.join(extra, total.core, core_layout)
        return grad_q.reshape(hq, hd, hd), grad_k.reshape(hk, hd, hd)

    in_specs = (
        P("dp", "seq", None),
        P("dp", "seq", None),
        P("dp", "seq", None),
        P("dp", "seq", None),
        P(),
        P(),
        P("dp", None),
    )
    return jax.shard_map(
        shards, mesh=mesh, in_specs=in_specs, out_specs=(P(), P()), check_vma=False
    )
```

```python
import functools
import math

import jax
import jax.numpy as jnp
from jax import lax
from jax.experimental import pallas as pl
from jax.experimental.pallas import tpu as pltpu
from jax.sharding import PartitionSpec as P

SPAN = 128
PAD = 8
WHOLE = 128
F32 = jnp.float32
BF16 = jnp.bfloat16
NN = (((1,), (0,)), ((), ()))
NT = (((1,), (1,)), ((), ()))
TN = (((0,), (0,)), ((), ()))
TT = (((0,), (1,)), ((), ()))


def dot(left, right, dims):
    return lax.dot_general(left, right, dims, preferred_element_type=F32)


def bounds(spans_ref, block):
    start, end, place = jnp.int32(0), jnp.int32(0), jnp.int32(0)
    for d in range(spans_ref.shape[1]):
        after = place + spans_ref[0, d]
        inside = jnp.logical_and(block >= place, block < after)
        start = jnp.where(inside, place, start)
        end = jnp.where(inside, after, end)
        place = after
    return start, end


def flag(condition):
    return jnp.where(condition, jnp.float32(1.0), jnp.float32(0.0))


def soft_pair(mapped, axis):
    up = jnp.exp(mapped - jnp.max(mapped, axis, keepdims=True))
    low = jnp.exp(jnp.min(mapped, axis, keepdims=True) - mapped)
    up = up * (1.0 / jnp.sum(up, axis, keepdims=True))
    low = low * (1.0 / jnp.sum(low, axis, keepdims=True))
    return up, low


def map_grad(up, low, grad_up, grad_low, axis):
    first = up * (grad_up - jnp.sum(up * grad_up, axis, keepdims=True))
    second = low * (grad_low - jnp.sum(low * grad_low, axis, keepdims=True))
    return (first - second).astype(BF16)


def tall_rows(row):
    return jnp.broadcast_to(row, (PAD, row.shape[1]))


def key_kernel(count, parts, spans_hbm, k_hbm, v_hbm, w_hbm, feat_ref, block_ref, *rest):
    tail_refs = rest[: len(parts)]
    spans_ref, k_ref, v_ref, w_ref, sems = rest[len(parts) :]
    pairs = [(spans_hbm, spans_ref), (k_hbm, k_ref), (w_hbm, w_ref), (v_hbm, v_ref)]
    copies = [pltpu.make_async_copy(a, b, sems.at[n]) for n, (a, b) in enumerate(pairs)]
    for copy in copies:
        copy.start()
    for copy in copies:
        copy.wait()
    width = w_ref.shape[-1]
    first = lax.axis_index("seq") * count
    starts = [bounds(spans_ref, first + c)[0] for c in range(count)]
    for (lo, hi), tail_ref in zip(parts, tail_refs):
        for i in range(lo, hi):
            cols = slice(i * width, (i + 1) * width)
            up, low = soft_pair(dot(k_ref[:, cols], w_ref[i], NN), -1)
            feat = jnp.concatenate([up, low], axis=-1).astype(BF16)
            feat_ref[i] = feat
            tail = None
            for c in range(count):
                rows = slice(c * SPAN, (c + 1) * SPAN)
                state = dot(v_ref[rows, cols], feat[rows], TN)
                norm = jnp.sum(feat[rows].astype(F32), axis=0, keepdims=True)
                both = jnp.concatenate([state, tall_rows(norm)], axis=0)
                block_ref[i, c] = both
                part = flag(starts[c] == starts[count - 1]) * both
                tail = part if tail is None else tail + part
            tall = tail.shape[0]
            tail_ref[(i - lo) * tall : (i - lo + 1) * tall] = tail


def join_kernel(count, hop, reverse, spans_ref, own_ref, came_ref, out_ref):
    place = lax.axis_index("seq")
    if reverse:
        _, end = bounds(spans_ref, place * count)
        keep = flag(end > (place + hop) * count)
    else:
        start, _ = bounds(spans_ref, place * count + count - 1)
        keep = flag(start < (place - hop + 1) * count)
    out_ref[...] = own_ref[...] + keep * came_ref[...]


def causal_mask(columns):
    t = lax.broadcasted_iota(jnp.int32, (SPAN, columns), 1) & (SPAN - 1)
    return lax.broadcasted_iota(jnp.int32, (SPAN, columns), 0) <= t


def early_kernel(part, count, group, *refs):
    q_ref, t_ref, v_ref, feat_k_ref, w_ref = refs[:5]
    up_ref, low_ref, feat_ref, num_ref, den_ref, tgt_ref = refs[5:]
    width = w_ref.shape[-1]
    causal = causal_mask(group * SPAN)
    for i in range(*part):
        k = i - part[0]
        for c in range(count):
            rows = slice(c * SPAN, (c + 1) * SPAN)
            cols = [slice(h * width, (h + 1) * width) for h in range(i * group, (i + 1) * group)]
            mapped = [dot(w_ref[i * group + h], q_ref[rows, cols[h]], TT) for h in range(group)]
            up, low = soft_pair(jnp.concatenate(mapped, axis=1), 0)
            up_ref[k, c] = up
            low_ref[k, c] = low
            feat = jnp.concatenate([up, low], axis=0).astype(BF16)
            feat_ref[k, c] = feat
            scores = jnp.where(causal, dot(feat_k_ref[i, rows], feat, NN), 0.0)
            den_ref[k, c] = tall_rows(jnp.sum(scores, 0, keepdims=True))
            vals = v_ref[rows, i * width : (i + 1) * width]
            num_ref[k, c] = dot(vals, scores.astype(BF16), TN)
            for h in range(group):
                tgt_ref[k, c, :, h * SPAN : (h + 1) * SPAN] = jnp.transpose(t_ref[rows, cols[h]])


def late_kernel(part, count, group, hops, coef, *refs):
    spans_ref, q_ref, v_ref, feat_k_ref, block_ref = refs[:5]
    up_ref, low_ref, feat_ref, num_ref, den_ref, tgt_ref = refs[5:11]
    came = refs[11 : 11 + hops]
    keep_ref, send_ref, head_ref, back_ref, inner_ref = refs[11 + hops :]
    width = tgt_ref.shape[2]
    tall = block_ref.shape[2]
    half = group // 2
    core = lax.axis_index("dp") & 1
    place = lax.axis_index("seq")
    first = place * count
    start_first, _ = bounds(spans_ref, first)
    causal = causal_mask(group * SPAN)
    for i in range(*part):
        k = i - part[0]
        grads, head = None, None
        for c in range(count):
            rows = slice(c * SPAN, (c + 1) * SPAN)
            start, _ = bounds(spans_ref, first + c)
            state = None
            for n in range(hops):
                near = start_first < (place - (1 << n) + 1) * count
                some = came[n][k * tall : (k + 1) * tall]
                some = flag(jnp.logical_and(near, start < first)) * some
                state = some if state is None else state + some
            for e in range(c):
                state = state + flag(start <= first + e) * block_ref[i, e]
            state = state.astype(BF16)
            feat_k = feat_k_ref[i, rows]
            feat = feat_ref[k, c]
            across = dot(state, feat, NN)
            numer = num_ref[k, c] + across[:SPAN]
            inverse = 1.0 / (den_ref[k, c, :1] + across[SPAN : SPAN + 1])
            output = numer * inverse
            d_out = coef * (output - tgt_ref[k, c].astype(F32))
            d_numer = (d_out * inverse).astype(BF16)
            d_denom = -jnp.sum(d_out * output, 0, keepdims=True) * inverse
            vals = v_ref[rows, i * width : (i + 1) * width]
            pairs = jnp.where(causal, dot(vals, d_numer, NN) + d_denom, 0.0).astype(BF16)
            mat = jnp.concatenate([feat_k, state[:SPAN]], axis=0)
            norm = jnp.transpose(state[SPAN:].astype(F32))[:, :1]
            d_feat = dot(mat, jnp.concatenate([pairs, d_numer], axis=0), TN) + norm * d_denom
            high = d_denom.astype(BF16)
            rest = d_denom - high.astype(F32)
            mid = rest.astype(BF16)
            low = (rest - mid.astype(F32)).astype(BF16)
            fill = jnp.zeros((2 * PAD - 3, high.shape[1]), BF16)
            left = jnp.concatenate([d_numer, pairs, high, mid, low, fill], axis=0)
            crossed = dot(left, feat, NT)
            at = 2 * SPAN
            norm_row = crossed[at : at + 1] + crossed[at + 1 : at + 2] + crossed[at + 2 : at + 3]
            back = jnp.concatenate([crossed[:SPAN], tall_rows(norm_row)], axis=0)
            back_ref[k, c] = back
            inner_ref[k, c] = crossed[SPAN:at]
            d_map = map_grad(up_ref[k, c], low_ref[k, c], d_feat[:width], d_feat[width:], 0)
            now = []
            for h in range(group):
                queries = q_ref[rows, (i * group + h) * width : (i * group + h + 1) * width]
                now.append(dot(d_map[:, h * SPAN : (h + 1) * SPAN], queries, NN))
            grads = now if grads is None else [a + b for a, b in zip(grads, now)]
            mine = flag(start == start_first) * back
            head = mine if head is None else head + mine
        head_ref[k * tall : (k + 1) * tall] = head
        for h in range(half):
            at = slice((k * half + h) * width, (k * half + h + 1) * width)
            keep_ref[at] = jnp.transpose(jnp.where(core == 0, grads[h], grads[half + h]))
            send_ref[at] = jnp.transpose(jnp.where(core == 0, grads[half + h], grads[h]))


def last_kernel(part, count, hops, *refs):
    spans_ref, k_ref, v_ref, w_ref, back_ref, inner_ref = refs[:6]
    came = refs[6 : 6 + hops]
    gk_ref = refs[6 + hops]
    width = w_ref.shape[-1]
    tall = back_ref.shape[2]
    place = lax.axis_index("seq")
    first = place * count
    _, end_last = bounds(spans_ref, first + count - 1)
    for i in range(*part):
        k = i - part[0]
        cols = slice(i * width, (i + 1) * width)
        keys = k_ref[:, cols]
        up, low = soft_pair(dot(keys, w_ref[i], NN), -1)
        grads = []
        for c in range(count):
            _, end = bounds(spans_ref, first + c)
            state = None
            for n in range(hops):
                near = end_last > (place + (1 << n)) * count
                some = came[n][k * tall : (k + 1) * tall]
                some = flag(jnp.logical_and(near, end > first + count)) * some
                state = some if state is None else state + some
            for e in range(c + 1, count):
                state = state + flag(end > first + e) * back_ref[k, e]
            norm = state[SPAN : SPAN + 1].astype(BF16).astype(F32)
            vals = v_ref[c * SPAN : (c + 1) * SPAN, cols]
            grads.append(inner_ref[k, c] + dot(vals, state[:SPAN].astype(BF16), NN) + norm)
        d_feat = jnp.concatenate(grads, axis=0)
        d_map = map_grad(up, low, d_feat[:, :width], d_feat[:, width:], -1)
        gk_ref[k * width : (k + 1) * width] = dot(keys, d_map, TN)


def cost(flops, moved):
    return pl.CostEstimate(flops=int(flops), bytes_accessed=int(moved), transcendentals=0)


SMEM = pl.BlockSpec(memory_space=pltpu.SMEM)
LIMIT = 32 << 20
PER_MICRO = 1e9


def local_call(body, out_shape, micros, *args, spans=None):
    first = [] if spans is None else [spans]
    return pl.pallas_call(
        body,
        out_shape=out_shape,
        in_specs=[SMEM] * len(first) + [pl.BlockSpec(memory_space=pltpu.VMEM)] * len(args),
        compiler_params=pltpu.CompilerParams(vmem_limit_bytes=LIMIT),
        cost_estimate=cost(micros * PER_MICRO, 0),
    )(*first, *args)


def index_in(stage):
    place = jnp.int32(0)
    for k, (axis, bit) in enumerate(stage):
        place = place + (((lax.axis_index(axis) >> bit) & 1) << k)
    return place


def split_kernel(stage, layout, *refs):
    pieces = 1 << len(stage)
    outs = refs[len(refs) - pieces :]
    mine = index_in(stage)
    for m, out in enumerate(outs):
        at, used = 0, 0
        for addends, rows in layout:
            size = rows // pieces
            start = 0 if pieces == 1 else pl.multiple_of((mine ^ m) * size, PAD)
            total = refs[used][pl.ds(start, size), :]
            for ref in refs[used + 1 : used + addends]:
                total = total + ref[pl.ds(start, size), :]
            out[at : at + size] = total
            at, used = at + size, used + addends


def join_pieces_kernel(stage, layout, *refs):
    pieces = 1 << len(stage)
    out = refs[pieces]
    mine = index_in(stage)
    for m in range(pieces):
        at, base = 0, 0
        for _, rows in layout:
            size = rows // pieces
            start = pl.multiple_of(base + (mine ^ m) * size, PAD)
            out[pl.ds(start, size), :] = refs[m][at : at + size]
            at, base = at + size, base + rows


def rows_of(rows, width):
    return jax.ShapeDtypeStruct((rows, width), F32)


class Summer:
    def __init__(self, n_dp, n_seq):
        self.n_dp, self.n_seq = n_dp, n_seq
        bits = [("dp", b) for b in range(1, n_dp.bit_length() - 1)]
        seq = [("seq", b) for b in range(n_seq.bit_length() - 1)]
        rest = bits[:1] + seq[:1] + seq[1:] + bits[1:]
        self.core = [("dp", 0)]
        self.stages = [rest[k : k + 2] for k in range(0, len(rest), 2)]

    def send(self, x, stage, mask):
        d_mask = sum(1 << b for k, (a, b) in enumerate(stage) if a == "dp" and mask >> k & 1)
        s_mask = sum(1 << b for k, (a, b) in enumerate(stage) if a == "seq" and mask >> k & 1)
        perm = [
            (d * self.n_seq + s, (d ^ d_mask) * self.n_seq + (s ^ s_mask))
            for d in range(self.n_dp)
            for s in range(self.n_seq)
        ]
        return lax.ppermute(x, ("dp", "seq"), perm)

    def split(self, groups, stage):
        pieces = 1 << len(stage)
        layout = [(len(g), g[0].shape[0]) for g in groups]
        size = sum(rows for _, rows in layout) // pieces
        width = groups[0][0].shape[1]
        out = local_call(
            functools.partial(split_kernel, stage, layout),
            [rows_of(size, width)] * pieces,
            0.4,
            *[a for g in groups for a in g],
        )
        return out, layout

    def join(self, x, stage, layout):
        came = [x] + [self.send(x, stage, m) for m in range(1, 1 << len(stage))]
        total = sum(rows for _, rows in layout)
        return local_call(
            functools.partial(join_pieces_kernel, stage, layout),
            rows_of(total, x.shape[1]),
            0.4,
            *came,
        )

    def scatter(self, groups, stage, whole=WHOLE):
        rows = [g[0].shape[0] for g in groups]
        if sum(rows) > whole and min(rows) >> len(stage) >= PAD:
            out, layout = self.split(groups, stage)
        else:
            whole, layout = self.split(groups, [])
            out, layout = [whole[0]] * (1 << len(stage)), None
        return [[out[0]] + [self.send(out[m], stage, m) for m in range(1, len(out))]], layout

    def gather(self, x, stage, layout):
        return x if layout is None else self.join(x, stage, layout)


def assemble_kernel(heads, half, own_ref, came_ref, out_ref):
    mine = lax.axis_index("dp") & 1
    for side, ref in enumerate((own_ref, came_ref)):
        for i in range(heads):
            start = pl.multiple_of((2 * i + (mine ^ side)) * half, PAD)
            out_ref[pl.ds(start, half), :] = ref[i * half : (i + 1) * half]


def solution(mesh):
    n_dp, n_seq = mesh.shape["dp"], mesh.shape["seq"]

    def shards(queries, keys, values, targets, q_map, k_map, doc_spans):
        hq, hd = q_map.shape[0], q_map.shape[1]
        hk = k_map.shape[0]
        group = hq // hk
        rows = queries.shape[1]
        count = rows // SPAN
        feats = 2 * hd
        tall = SPAN + PAD
        coef = 2.0 / math.sqrt(n_dp * n_seq * rows * hd)
        most = (3 * n_seq * count) // 8
        before = min(n_seq - 1, -(-(most - 1) // count))
        hops = max(1, before.bit_length())
        q2, t2 = queries[0], targets[0]
        k2, v2 = keys[0], values[0]
        parts = [(0, hk // 2), (hk // 2, hk)]
        array = jax.ShapeDtypeStruct
        out = pl.pallas_call(
            functools.partial(key_kernel, count, parts),
            out_shape=[array((hk, rows, feats), BF16), array((hk, count, tall, feats), F32)]
            + [rows_of((hi - lo) * tall, feats) for lo, hi in parts],
            in_specs=[pl.BlockSpec(memory_space=pl.ANY)] * 4,
            scratch_shapes=[
                pltpu.SMEM(doc_spans.shape, jnp.int32),
                pltpu.VMEM(k2.shape, BF16),
                pltpu.VMEM(v2.shape, BF16),
                pltpu.VMEM(k_map.shape, BF16),
                pltpu.SemaphoreType.DMA((4,)),
            ],
            compiler_params=pltpu.CompilerParams(vmem_limit_bytes=LIMIT),
            cost_estimate=cost(3 * PER_MICRO, 0),
        )(doc_spans, k2, v2, k_map)
        feat_k, blocks, tails = out[0], out[1], out[2:]

        def shift(own, hop, reverse):
            step = -hop if reverse else hop
            ring = [(i, (i + step) % n_seq) for i in range(n_seq)]
            return lax.ppermute(own, "seq", ring)

        def join(own, got, hop, reverse):
            return local_call(
                functools.partial(join_kernel, count, hop, reverse),
                rows_of(*own.shape),
                0.6,
                own,
                got,
                spans=doc_spans,
            )

        def exchange(own, reverse, start=0):
            came = []
            for k in range(start, hops):
                came.append(shift(own, 1 << k, reverse))
                if k < hops - 1:
                    own = join(own, came[-1], 1 << k, reverse)
            return came

        def early(part):
            wide = lambda r, dtype: array((part[1] - part[0], count, r, group * SPAN), dtype)
            return local_call(
                functools.partial(early_kernel, part, count, group),
                [wide(hd, F32), wide(hd, F32), wide(feats, BF16), wide(hd, F32), wide(PAD, F32)]
                + [wide(hd, BF16)],
                3.0,
                q2,
                t2,
                v2,
                feat_k,
                q_map,
            )

        def late(part, ready, came):
            heads = part[1] - part[0]
            return local_call(
                functools.partial(late_kernel, part, count, group, hops, coef),
                [rows_of(heads * group * hd // 2, hd)] * 2
                + [rows_of(heads * tall, feats)]
                + [array((heads, count, tall, feats), F32), array((heads, count, SPAN, feats), F32)],
                6.0,
                q2,
                v2,
                feat_k,
                blocks,
                *ready,
                *came,
                spans=doc_spans,
            )

        def last(part, back, inner, came):
            return local_call(
                functools.partial(last_kernel, part, count, hops),
                rows_of((part[1] - part[0]) * hd, hd),
                1.5,
                k2,
                v2,
                k_map,
                back,
                inner,
                *came,
                spans=doc_spans,
            )

        total = Summer(n_dp, n_seq)
        came = [exchange(t, False) for t in tails]
        ready = [early(p) for p in parts]
        first = late(parts[0], ready[0], came[0])
        back_one = [shift(first[2], 1, True)]
        core_one = total.send(first[1], total.core, 1)
        second = late(parts[1], ready[1], came[1])
        core_one, *second = lax.optimization_barrier((core_one, *second))
        back_two = [shift(second[2], 1, True)]
        core_two = total.send(second[1], total.core, 1)
        groups, layout = total.scatter([[first[0], core_one], [second[0], core_two]], total.stages[0])
        layouts = [layout]
        ends = [
            join(own[2], back[0], 1, True) if hops > 1 else back[0]
            for own, back in ((first, back_one), (second, back_two))
        ]
        if hops > 1:
            back_two += exchange(ends[1], True, 1)
            back_one += exchange(ends[0], True, 1)
        groups, ends = lax.optimization_barrier((groups, ends))
        for stage in total.stages[1:]:
            groups, layout = total.scatter(groups, stage)
            layouts.append(layout)
        x = total.split(groups, [])[0][0]
        gk = [
            last(p, m[3], m[4], b)
            for p, m, b in zip(parts, (first, second), (back_one, back_two))
        ]
        out, core_layout = total.split([[g] for g in gk], total.core)
        extra = [[out[0], total.send(out[1], total.core, 1)]]
        x, extra = lax.optimization_barrier((x, extra))
        for stage, layout in reversed(list(zip(total.stages[1:], layouts[1:]))):
            x = total.gather(x, stage, layout)
        extra, layout = total.scatter(extra, total.stages[0], 2 * WHOLE)
        extra_layouts = [layout]
        x, extra = lax.optimization_barrier((x, extra))
        x = total.gather(x, total.stages[0], layouts[0])
        for stage in total.stages[1:]:
            extra, layout = total.scatter(extra, stage, 2 * WHOLE)
            extra_layouts.append(layout)
        extra = total.split(extra, [])[0][0]
        for stage, layout in reversed(list(zip(total.stages, extra_layouts))):
            extra = total.gather(extra, stage, layout)
        x, extra = lax.optimization_barrier((x, extra))
        halves = [x, total.send(x, total.core, 1)]
        grad_q = local_call(
            functools.partial(assemble_kernel, hk, group * hd // 2),
            rows_of(hq * hd, hd),
            1.0,
            *halves,
        )
        grad_k = total.join(extra, total.core, core_layout)
        return grad_q.reshape(hq, hd, hd), grad_k.reshape(hk, hd, hd)

    in_specs = (
        P("dp", "seq", None),
        P("dp", "seq", None),
        P("dp", "seq", None),
        P("dp", "seq", None),
        P(),
        P(),
        P("dp", None),
    )
    return jax.shard_map(
        shards, mesh=mesh, in_specs=in_specs, out_specs=(P(), P()), check_vma=False
    )
```

```python
import functools
import math

import jax
import jax.numpy as jnp
from jax import lax
from jax.experimental import pallas as pl
from jax.experimental.pallas import tpu as pltpu
from jax.sharding import PartitionSpec as P

SPAN = 128
PAD = 8
WHOLE = 128
F32 = jnp.float32
BF16 = jnp.bfloat16
NN = (((1,), (0,)), ((), ()))
NT = (((1,), (1,)), ((), ()))
TN = (((0,), (0,)), ((), ()))
TT = (((0,), (1,)), ((), ()))


def dot(left, right, dims):
    return lax.dot_general(left, right, dims, preferred_element_type=F32)


def bounds(spans_ref, block):
    start, end, place = jnp.int32(0), jnp.int32(0), jnp.int32(0)
    for d in range(spans_ref.shape[1]):
        after = place + spans_ref[0, d]
        inside = jnp.logical_and(block >= place, block < after)
        start = jnp.where(inside, place, start)
        end = jnp.where(inside, after, end)
        place = after
    return start, end


def flag(condition):
    return jnp.where(condition, jnp.float32(1.0), jnp.float32(0.0))


def soft_pair(mapped, axis):
    up = jnp.exp(mapped - jnp.max(mapped, axis, keepdims=True))
    low = jnp.exp(jnp.min(mapped, axis, keepdims=True) - mapped)
    up = up * (1.0 / jnp.sum(up, axis, keepdims=True))
    low = low * (1.0 / jnp.sum(low, axis, keepdims=True))
    return up, low


def map_grad(up, low, grad_up, grad_low, axis):
    first = up * (grad_up - jnp.sum(up * grad_up, axis, keepdims=True))
    second = low * (grad_low - jnp.sum(low * grad_low, axis, keepdims=True))
    return (first - second).astype(BF16)


def tall_rows(row):
    return jnp.broadcast_to(row, (PAD, row.shape[1]))


def key_kernel(count, parts, width, spans_ref, packed_ref, feat_ref, block_ref, *tail_refs):
    total = parts[-1][1] * width
    stack = packed_ref.shape[0] // width
    first = lax.axis_index("seq") * count
    starts = [bounds(spans_ref, first + c)[0] for c in range(count)]
    for (lo, hi), tail_ref in zip(parts, tail_refs):
        for i in range(lo, hi):
            cols = slice(i * width, (i + 1) * width)
            at = 2 * total + i // stack * width
            weight = packed_ref[i % stack * width : (i % stack + 1) * width, at : at + width]
            up, low = soft_pair(dot(packed_ref[:, cols], weight, NN), -1)
            feat = jnp.concatenate([up, low], axis=-1).astype(BF16)
            feat_ref[i] = feat
            tail = None
            for c in range(count):
                rows = slice(c * SPAN, (c + 1) * SPAN)
                vals = packed_ref[rows, total + i * width : total + (i + 1) * width]
                state = dot(vals, feat[rows], TN)
                norm = jnp.sum(feat[rows].astype(F32), axis=0, keepdims=True)
                both = jnp.concatenate([state, tall_rows(norm)], axis=0)
                block_ref[i, c] = both
                part = flag(starts[c] == starts[count - 1]) * both
                tail = part if tail is None else tail + part
            tall = tail.shape[0]
            tail_ref[(i - lo) * tall : (i - lo + 1) * tall] = tail


def join_kernel(count, hop, reverse, spans_ref, own_ref, came_ref, out_ref):
    place = lax.axis_index("seq")
    if reverse:
        _, end = bounds(spans_ref, place * count)
        keep = flag(end > (place + hop) * count)
    else:
        start, _ = bounds(spans_ref, place * count + count - 1)
        keep = flag(start < (place - hop + 1) * count)
    out_ref[...] = own_ref[...] + keep * came_ref[...]


def causal_mask(columns):
    t = lax.broadcasted_iota(jnp.int32, (SPAN, columns), 1) & (SPAN - 1)
    return lax.broadcasted_iota(jnp.int32, (SPAN, columns), 0) <= t


def early_kernel(part, count, group, *refs):
    q_ref, t_ref, v_ref, feat_k_ref, w_ref = refs[:5]
    up_ref, low_ref, feat_ref, num_ref, den_ref, tgt_ref = refs[5:]
    width = w_ref.shape[-1]
    causal = causal_mask(group * SPAN)
    for i in range(*part):
        k = i - part[0]
        for c in range(count):
            rows = slice(c * SPAN, (c + 1) * SPAN)
            cols = [slice(h * width, (h + 1) * width) for h in range(i * group, (i + 1) * group)]
            mapped = [dot(w_ref[i * group + h], q_ref[rows, cols[h]], TT) for h in range(group)]
            up, low = soft_pair(jnp.concatenate(mapped, axis=1), 0)
            up_ref[k, c] = up
            low_ref[k, c] = low
            feat = jnp.concatenate([up, low], axis=0).astype(BF16)
            feat_ref[k, c] = feat
            scores = jnp.where(causal, dot(feat_k_ref[i, rows], feat, NN), 0.0)
            den_ref[k, c] = tall_rows(jnp.sum(scores, 0, keepdims=True))
            vals = v_ref[rows, i * width : (i + 1) * width]
            num_ref[k, c] = dot(vals, scores.astype(BF16), TN)
            for h in range(group):
                tgt_ref[k, c, :, h * SPAN : (h + 1) * SPAN] = jnp.transpose(t_ref[rows, cols[h]])


def late_kernel(part, count, group, hops, coef, *refs):
    spans_ref, q_ref, v_ref, feat_k_ref, block_ref = refs[:5]
    up_ref, low_ref, feat_ref, num_ref, den_ref, tgt_ref = refs[5:11]
    came = refs[11 : 11 + hops]
    keep_ref, send_ref, head_ref, back_ref, inner_ref = refs[11 + hops :]
    width = tgt_ref.shape[2]
    tall = block_ref.shape[2]
    half = group // 2
    core = lax.axis_index("dp") & 1
    place = lax.axis_index("seq")
    first = place * count
    start_first, _ = bounds(spans_ref, first)
    causal = causal_mask(group * SPAN)
    for i in range(*part):
        k = i - part[0]
        grads, head = None, None
        for c in range(count):
            rows = slice(c * SPAN, (c + 1) * SPAN)
            start, _ = bounds(spans_ref, first + c)
            state = None
            for n in range(hops):
                near = start_first < (place - (1 << n) + 1) * count
                some = came[n][k * tall : (k + 1) * tall]
                some = flag(jnp.logical_and(near, start < first)) * some
                state = some if state is None else state + some
            for e in range(c):
                state = state + flag(start <= first + e) * block_ref[i, e]
            state = state.astype(BF16)
            feat_k = feat_k_ref[i, rows]
            feat = feat_ref[k, c]
            across = dot(state, feat, NN)
            numer = num_ref[k, c] + across[:SPAN]
            inverse = 1.0 / (den_ref[k, c, :1] + across[SPAN : SPAN + 1])
            output = numer * inverse
            d_out = coef * (output - tgt_ref[k, c].astype(F32))
            d_numer = (d_out * inverse).astype(BF16)
            d_denom = -jnp.sum(d_out * output, 0, keepdims=True) * inverse
            vals = v_ref[rows, i * width : (i + 1) * width]
            pairs = jnp.where(causal, dot(vals, d_numer, NN) + d_denom, 0.0).astype(BF16)
            mat = jnp.concatenate([feat_k, state[:SPAN]], axis=0)
            norm = jnp.transpose(state[SPAN:].astype(F32))[:, :1]
            d_feat = dot(mat, jnp.concatenate([pairs, d_numer], axis=0), TN) + norm * d_denom
            high = d_denom.astype(BF16)
            rest = d_denom - high.astype(F32)
            mid = rest.astype(BF16)
            low = (rest - mid.astype(F32)).astype(BF16)
            fill = jnp.zeros((2 * PAD - 3, high.shape[1]), BF16)
            left = jnp.concatenate([d_numer, pairs, high, mid, low, fill], axis=0)
            crossed = dot(left, feat, NT)
            at = 2 * SPAN
            norm_row = crossed[at : at + 1] + crossed[at + 1 : at + 2] + crossed[at + 2 : at + 3]
            back = jnp.concatenate([crossed[:SPAN], tall_rows(norm_row)], axis=0)
            back_ref[k, c] = back
            inner_ref[k, c] = crossed[SPAN:at]
            d_map = map_grad(up_ref[k, c], low_ref[k, c], d_feat[:width], d_feat[width:], 0)
            now = []
            for h in range(group):
                queries = q_ref[rows, (i * group + h) * width : (i * group + h + 1) * width]
                now.append(dot(d_map[:, h * SPAN : (h + 1) * SPAN], queries, NN))
            grads = now if grads is None else [a + b for a, b in zip(grads, now)]
            mine = flag(start == start_first) * back
            head = mine if head is None else head + mine
        head_ref[k * tall : (k + 1) * tall] = head
        for h in range(half):
            at = slice((k * half + h) * width, (k * half + h + 1) * width)
            keep_ref[at] = jnp.transpose(jnp.where(core == 0, grads[h], grads[half + h]))
            send_ref[at] = jnp.transpose(jnp.where(core == 0, grads[half + h], grads[h]))


def last_kernel(part, count, hops, *refs):
    spans_ref, k_ref, v_ref, w_ref, back_ref, inner_ref = refs[:6]
    came = refs[6 : 6 + hops]
    gk_ref = refs[6 + hops]
    width = w_ref.shape[-1]
    tall = back_ref.shape[2]
    place = lax.axis_index("seq")
    first = place * count
    _, end_last = bounds(spans_ref, first + count - 1)
    for i in range(*part):
        k = i - part[0]
        cols = slice(i * width, (i + 1) * width)
        keys = k_ref[:, cols]
        up, low = soft_pair(dot(keys, w_ref[i], NN), -1)
        grads = []
        for c in range(count):
            _, end = bounds(spans_ref, first + c)
            state = None
            for n in range(hops):
                near = end_last > (place + (1 << n)) * count
                some = came[n][k * tall : (k + 1) * tall]
                some = flag(jnp.logical_and(near, end > first + count)) * some
                state = some if state is None else state + some
            for e in range(c + 1, count):
                state = state + flag(end > first + e) * back_ref[k, e]
            norm = state[SPAN : SPAN + 1].astype(BF16).astype(F32)
            vals = v_ref[c * SPAN : (c + 1) * SPAN, cols]
            grads.append(inner_ref[k, c] + dot(vals, state[:SPAN].astype(BF16), NN) + norm)
        d_feat = jnp.concatenate(grads, axis=0)
        d_map = map_grad(up, low, d_feat[:, :width], d_feat[:, width:], -1)
        gk_ref[k * width : (k + 1) * width] = dot(keys, d_map, TN)


def cost(flops, moved):
    return pl.CostEstimate(flops=int(flops), bytes_accessed=int(moved), transcendentals=0)


SMEM = pl.BlockSpec(memory_space=pltpu.SMEM)
LIMIT = 32 << 20
PER_MICRO = 1e9


def local_call(body, out_shape, micros, *args, spans=None):
    first = [] if spans is None else [spans]
    return pl.pallas_call(
        body,
        out_shape=out_shape,
        in_specs=[SMEM] * len(first) + [pl.BlockSpec(memory_space=pltpu.VMEM)] * len(args),
        compiler_params=pltpu.CompilerParams(vmem_limit_bytes=LIMIT),
        cost_estimate=cost(micros * PER_MICRO, 0),
    )(*first, *args)


def index_in(stage):
    place = jnp.int32(0)
    for k, (axis, bit) in enumerate(stage):
        place = place + (((lax.axis_index(axis) >> bit) & 1) << k)
    return place


def split_kernel(stage, layout, *refs):
    pieces = 1 << len(stage)
    outs = refs[len(refs) - pieces :]
    mine = index_in(stage)
    for m, out in enumerate(outs):
        at, used = 0, 0
        for addends, rows in layout:
            size = rows // pieces
            start = 0 if pieces == 1 else pl.multiple_of((mine ^ m) * size, PAD)
            total = refs[used][pl.ds(start, size), :]
            for ref in refs[used + 1 : used + addends]:
                total = total + ref[pl.ds(start, size), :]
            out[at : at + size] = total
            at, used = at + size, used + addends


def join_pieces_kernel(stage, layout, *refs):
    pieces = 1 << len(stage)
    out = refs[pieces]
    mine = index_in(stage)
    for m in range(pieces):
        at, base = 0, 0
        for _, rows in layout:
            size = rows // pieces
            start = pl.multiple_of(base + (mine ^ m) * size, PAD)
            out[pl.ds(start, size), :] = refs[m][at : at + size]
            at, base = at + size, base + rows


def rows_of(rows, width):
    return jax.ShapeDtypeStruct((rows, width), F32)


class Summer:
    def __init__(self, n_dp, n_seq):
        self.n_dp, self.n_seq = n_dp, n_seq
        bits = [("dp", b) for b in range(1, n_dp.bit_length() - 1)]
        seq = [("seq", b) for b in range(n_seq.bit_length() - 1)]
        rest = bits[:1] + seq[:1] + seq[1:] + bits[1:]
        self.core = [("dp", 0)]
        self.stages = [rest[k : k + 2] for k in range(0, len(rest), 2)]

    def send(self, x, stage, mask):
        d_mask = sum(1 << b for k, (a, b) in enumerate(stage) if a == "dp" and mask >> k & 1)
        s_mask = sum(1 << b for k, (a, b) in enumerate(stage) if a == "seq" and mask >> k & 1)
        perm = [
            (d * self.n_seq + s, (d ^ d_mask) * self.n_seq + (s ^ s_mask))
            for d in range(self.n_dp)
            for s in range(self.n_seq)
        ]
        return lax.ppermute(x, ("dp", "seq"), perm)

    def split(self, groups, stage):
        pieces = 1 << len(stage)
        layout = [(len(g), g[0].shape[0]) for g in groups]
        size = sum(rows for _, rows in layout) // pieces
        width = groups[0][0].shape[1]
        out = local_call(
            functools.partial(split_kernel, stage, layout),
            [rows_of(size, width)] * pieces,
            0.4,
            *[a for g in groups for a in g],
        )
        return out, layout

    def join(self, x, stage, layout):
        came = [x] + [self.send(x, stage, m) for m in range(1, 1 << len(stage))]
        total = sum(rows for _, rows in layout)
        return local_call(
            functools.partial(join_pieces_kernel, stage, layout),
            rows_of(total, x.shape[1]),
            0.4,
            *came,
        )

    def scatter(self, groups, stage, whole=WHOLE):
        rows = [g[0].shape[0] for g in groups]
        if sum(rows) > whole and min(rows) >> len(stage) >= PAD:
            out, layout = self.split(groups, stage)
        else:
            whole, layout = self.split(groups, [])
            out, layout = [whole[0]] * (1 << len(stage)), None
        return [[out[0]] + [self.send(out[m], stage, m) for m in range(1, len(out))]], layout

    def gather(self, x, stage, layout):
        return x if layout is None else self.join(x, stage, layout)


def assemble_kernel(heads, half, stage, layout, own_ref, came_ref, key_own, key_came, out_ref, key_ref):
    join_pieces_kernel(stage, layout, key_own, key_came, key_ref)
    mine = lax.axis_index("dp") & 1
    for side, ref in enumerate((own_ref, came_ref)):
        for i in range(heads):
            start = pl.multiple_of((2 * i + (mine ^ side)) * half, PAD)
            out_ref[pl.ds(start, half), :] = ref[i * half : (i + 1) * half]


def solution(mesh):
    n_dp, n_seq = mesh.shape["dp"], mesh.shape["seq"]

    def shards(queries, keys, values, targets, q_map, k_map, doc_spans):
        hq, hd = q_map.shape[0], q_map.shape[1]
        hk = k_map.shape[0]
        group = hq // hk
        rows = queries.shape[1]
        count = rows // SPAN
        feats = 2 * hd
        tall = SPAN + PAD
        coef = 2.0 / math.sqrt(n_dp * n_seq * rows * hd)
        most = (3 * n_seq * count) // 8
        before = min(n_seq - 1, -(-(most - 1) // count))
        hops = max(1, before.bit_length())
        q2, t2 = queries[0], targets[0]
        k2, v2 = keys[0], values[0]
        parts = [(0, hk // 2), (hk // 2, hk)]
        array = jax.ShapeDtypeStruct
        stack = rows // hd
        weights = jnp.pad(k_map, ((0, -hk % stack), (0, 0), (0, 0)))
        weights = [weights[i : i + stack].reshape(rows, hd) for i in range(0, hk, stack)]
        out = local_call(
            functools.partial(key_kernel, count, parts, hd),
            [array((hk, rows, feats), BF16), array((hk, count, tall, feats), F32)]
            + [rows_of((hi - lo) * tall, feats) for lo, hi in parts],
            3.0,
            jnp.concatenate([k2, v2] + weights, axis=1),
            spans=doc_spans,
        )
        feat_k, blocks, tails = out[0], out[1], out[2:]

        def shift(own, hop, reverse):
            step = -hop if reverse else hop
            ring = [(i, (i + step) % n_seq) for i in range(n_seq)]
            return lax.ppermute(own, "seq", ring)

        def join(own, got, hop, reverse):
            return local_call(
                functools.partial(join_kernel, count, hop, reverse),
                rows_of(*own.shape),
                0.6,
                own,
                got,
                spans=doc_spans,
            )

        def exchange(own, reverse, start=0):
            came = []
            for k in range(start, hops):
                came.append(shift(own, 1 << k, reverse))
                if k < hops - 1:
                    own = join(own, came[-1], 1 << k, reverse)
            return came

        def early(part):
            wide = lambda r, dtype: array((part[1] - part[0], count, r, group * SPAN), dtype)
            return local_call(
                functools.partial(early_kernel, part, count, group),
                [wide(hd, F32), wide(hd, F32), wide(feats, BF16), wide(hd, F32), wide(PAD, F32)]
                + [wide(hd, BF16)],
                1.5,
                q2,
                t2,
                v2,
                feat_k,
                q_map,
            )

        def late(part, ready, came):
            heads = part[1] - part[0]
            return local_call(
                functools.partial(late_kernel, part, count, group, hops, coef),
                [rows_of(heads * group * hd // 2, hd)] * 2
                + [rows_of(heads * tall, feats)]
                + [array((heads, count, tall, feats), F32), array((heads, count, SPAN, feats), F32)],
                6,
                q2,
                v2,
                feat_k,
                blocks,
                *ready,
                *came,
                spans=doc_spans,
            )

        def last(part, back, inner, came):
            return local_call(
                functools.partial(last_kernel, part, count, hops),
                rows_of((part[1] - part[0]) * hd, hd),
                0.5,
                k2,
                v2,
                k_map,
                back,
                inner,
                *came,
                spans=doc_spans,
            )

        total = Summer(n_dp, n_seq)
        came = [exchange(t, False) for t in tails]
        ready = [early(p) for p in parts]
        first = late(parts[0], ready[0], came[0])
        back_one = [shift(first[2], 1, True)]
        core_one = total.send(first[1], total.core, 1)
        second = late(parts[1], ready[1], came[1])
        core_one, *second = lax.optimization_barrier((core_one, *second))
        back_two = [shift(second[2], 1, True)]
        core_two = total.send(second[1], total.core, 1)
        groups, layout = total.scatter([[first[0], core_one], [second[0], core_two]], total.stages[0])
        layouts = [layout]
        ends = [
            join(own[2], back[0], 1, True) if hops > 1 else back[0]
            for own, back in ((first, back_one), (second, back_two))
        ]
        if hops > 1:
            back_two += exchange(ends[1], True, 1)
            back_one += exchange(ends[0], True, 1)
        groups, ends = lax.optimization_barrier((groups, ends))
        for stage in total.stages[1:]:
            groups, layout = total.scatter(groups, stage)
            layouts.append(layout)
        x = total.split(groups, [])[0][0]
        gk = [
            last(p, m[3], m[4], b)
            for p, m, b in zip(parts, (first, second), (back_one, back_two))
        ]
        out, core_layout = total.split([[g] for g in gk], total.core)
        extra = [[out[0], total.send(out[1], total.core, 1)]]
        extra, layout = total.scatter(extra, total.stages[0], 2 * WHOLE)
        extra_layouts = [layout]
        x, extra = lax.optimization_barrier((x, extra))
        for stage, layout in reversed(list(zip(total.stages, layouts))):
            x = total.gather(x, stage, layout)
        for stage in total.stages[1:]:
            extra, layout = total.scatter(extra, stage, 2 * WHOLE)
            extra_layouts.append(layout)
        extra = total.split(extra, [])[0][0]
        for stage, layout in reversed(list(zip(total.stages, extra_layouts))):
            extra = total.gather(extra, stage, layout)
        x, extra = lax.optimization_barrier((x, extra))
        halves = [x, total.send(x, total.core, 1), extra, total.send(extra, total.core, 1)]
        grad_q, grad_k = local_call(
            functools.partial(assemble_kernel, hk, group * hd // 2, total.core, core_layout),
            [rows_of(hq * hd, hd), rows_of(hk * hd, hd)],
            1.0,
            *halves,
        )
        return grad_q.reshape(hq, hd, hd), grad_k.reshape(hk, hd, hd)

    in_specs = (
        P("dp", "seq", None),
        P("dp", "seq", None),
        P("dp", "seq", None),
        P("dp", "seq", None),
        P(),
        P(),
        P("dp", None),
    )
    return jax.shard_map(
        shards, mesh=mesh, in_specs=in_specs, out_specs=(P(), P()), check_vma=False
    )
```

```python
import functools
import math

import jax
import jax.numpy as jnp
from jax import lax
from jax.experimental import pallas as pl
from jax.experimental.pallas import tpu as pltpu
from jax.sharding import PartitionSpec as P

SPAN = 128
PAD = 8
WHOLE = 128
F32 = jnp.float32
BF16 = jnp.bfloat16
NN = (((1,), (0,)), ((), ()))
NT = (((1,), (1,)), ((), ()))
TN = (((0,), (0,)), ((), ()))
TT = (((0,), (1,)), ((), ()))


def dot(left, right, dims):
    return lax.dot_general(left, right, dims, preferred_element_type=F32)


def bounds(spans_ref, block):
    start, end, place = jnp.int32(0), jnp.int32(0), jnp.int32(0)
    for d in range(spans_ref.shape[1]):
        after = place + spans_ref[0, d]
        inside = jnp.logical_and(block >= place, block < after)
        start = jnp.where(inside, place, start)
        end = jnp.where(inside, after, end)
        place = after
    return start, end


def flag(condition):
    return jnp.where(condition, jnp.float32(1.0), jnp.float32(0.0))


def soft_pair(mapped, axis):
    up = jnp.exp(mapped - jnp.max(mapped, axis, keepdims=True))
    low = jnp.exp(jnp.min(mapped, axis, keepdims=True) - mapped)
    up = up * (1.0 / jnp.sum(up, axis, keepdims=True))
    low = low * (1.0 / jnp.sum(low, axis, keepdims=True))
    return up, low


def map_grad(up, low, grad_up, grad_low, axis):
    first = up * (grad_up - jnp.sum(up * grad_up, axis, keepdims=True))
    second = low * (grad_low - jnp.sum(low * grad_low, axis, keepdims=True))
    return (first - second).astype(BF16)


def tall_rows(row):
    return jnp.broadcast_to(row, (PAD, row.shape[1]))


def key_kernel(count, parts, width, spans_ref, packed_ref, feat_ref, block_ref, *tail_refs):
    total = parts[-1][1] * width
    stack = packed_ref.shape[0] // width
    first = lax.axis_index("seq") * count
    starts = [bounds(spans_ref, first + c)[0] for c in range(count)]
    for (lo, hi), tail_ref in zip(parts, tail_refs):
        for i in range(lo, hi):
            cols = slice(i * width, (i + 1) * width)
            at = 2 * total + i // stack * width
            weight = packed_ref[i % stack * width : (i % stack + 1) * width, at : at + width]
            up, low = soft_pair(dot(packed_ref[:, cols], weight, NN), -1)
            feat = jnp.concatenate([up, low], axis=-1).astype(BF16)
            feat_ref[i] = feat
            tail = None
            for c in range(count):
                rows = slice(c * SPAN, (c + 1) * SPAN)
                vals = packed_ref[rows, total + i * width : total + (i + 1) * width]
                state = dot(vals, feat[rows], TN)
                norm = jnp.sum(feat[rows].astype(F32), axis=0, keepdims=True)
                both = jnp.concatenate([state, tall_rows(norm)], axis=0)
                block_ref[i, c] = both
                part = flag(starts[c] == starts[count - 1]) * both
                tail = part if tail is None else tail + part
            tall = tail.shape[0]
            tail_ref[(i - lo) * tall : (i - lo + 1) * tall] = tail


def join_kernel(count, hop, reverse, spans_ref, own_ref, came_ref, out_ref):
    place = lax.axis_index("seq")
    if reverse:
        _, end = bounds(spans_ref, place * count)
        keep = flag(end > (place + hop) * count)
    else:
        start, _ = bounds(spans_ref, place * count + count - 1)
        keep = flag(start < (place - hop + 1) * count)
    out_ref[...] = own_ref[...] + keep * came_ref[...]


def causal_mask(columns):
    t = lax.broadcasted_iota(jnp.int32, (SPAN, columns), 1) & (SPAN - 1)
    return lax.broadcasted_iota(jnp.int32, (SPAN, columns), 0) <= t


def early_kernel(part, count, group, *refs):
    q_ref, t_ref, v_ref, feat_k_ref, w_ref = refs[:5]
    up_ref, low_ref, feat_ref, num_ref, den_ref, tgt_ref = refs[5:]
    width = w_ref.shape[-1]
    causal = causal_mask(group * SPAN)
    for i in range(*part):
        k = i - part[0]
        for c in range(count):
            rows = slice(c * SPAN, (c + 1) * SPAN)
            cols = [slice(h * width, (h + 1) * width) for h in range(i * group, (i + 1) * group)]
            mapped = [dot(w_ref[i * group + h], q_ref[rows, cols[h]], TT) for h in range(group)]
            up, low = soft_pair(jnp.concatenate(mapped, axis=1), 0)
            up_ref[k, c] = up
            low_ref[k, c] = low
            feat = jnp.concatenate([up, low], axis=0).astype(BF16)
            feat_ref[k, c] = feat
            scores = jnp.where(causal, dot(feat_k_ref[i, rows], feat, NN), 0.0)
            den_ref[k, c] = tall_rows(jnp.sum(scores, 0, keepdims=True))
            vals = v_ref[rows, i * width : (i + 1) * width]
            num_ref[k, c] = dot(vals, scores.astype(BF16), TN)
            for h in range(group):
                tgt_ref[k, c, :, h * SPAN : (h + 1) * SPAN] = jnp.transpose(t_ref[rows, cols[h]])


def late_kernel(part, count, group, hops, coef, *refs):
    spans_ref, q_ref, v_ref, feat_k_ref, block_ref = refs[:5]
    up_ref, low_ref, feat_ref, num_ref, den_ref, tgt_ref = refs[5:11]
    came = refs[11 : 11 + hops]
    keep_ref, send_ref, head_ref, back_ref, inner_ref = refs[11 + hops :]
    width = tgt_ref.shape[2]
    tall = block_ref.shape[2]
    half = group // 2
    core = lax.axis_index("dp") & 1
    place = lax.axis_index("seq")
    first = place * count
    start_first, _ = bounds(spans_ref, first)
    causal = causal_mask(group * SPAN)
    for i in range(*part):
        k = i - part[0]
        grads, head = None, None
        for c in range(count):
            rows = slice(c * SPAN, (c + 1) * SPAN)
            start, _ = bounds(spans_ref, first + c)
            state = None
            for n in range(hops):
                near = start_first < (place - (1 << n) + 1) * count
                some = came[n][k * tall : (k + 1) * tall]
                some = flag(jnp.logical_and(near, start < first)) * some
                state = some if state is None else state + some
            for e in range(c):
                state = state + flag(start <= first + e) * block_ref[i, e]
            state = jnp.concatenate([state, state[SPAN:]], axis=0).astype(BF16)
            feat_k = feat_k_ref[i, rows]
            feat = feat_ref[k, c]
            across = dot(state, feat, NN)
            numer = num_ref[k, c] + across[:SPAN]
            inverse = 1.0 / (den_ref[k, c, :1] + across[SPAN : SPAN + 1])
            output = numer * inverse
            d_out = coef * (output - tgt_ref[k, c].astype(F32))
            d_numer = (d_out * inverse).astype(BF16)
            d_denom = -jnp.sum(d_out * output, 0, keepdims=True) * inverse
            vals = v_ref[rows, i * width : (i + 1) * width]
            pairs = jnp.where(causal, dot(vals, d_numer, NN) + d_denom, 0.0).astype(BF16)
            mat = jnp.concatenate([feat_k, state[:SPAN]], axis=0)
            norm = jnp.transpose(state[SPAN:].astype(F32))[:, :1]
            d_feat = dot(mat, jnp.concatenate([pairs, d_numer], axis=0), TN) + norm * d_denom
            high = d_denom.astype(BF16)
            rest = d_denom - high.astype(F32)
            mid = rest.astype(BF16)
            low = (rest - mid.astype(F32)).astype(BF16)
            three = [high.astype(F32), mid.astype(F32), low.astype(F32)]
            three.append(jnp.zeros((2 * PAD - 3, high.shape[1]), F32))
            three = jnp.concatenate(three, axis=0).astype(BF16)
            left = jnp.concatenate([d_numer, pairs, three], axis=0)
            crossed = dot(left, feat, NT)
            at = 2 * SPAN
            norm_row = crossed[at : at + 1] + crossed[at + 1 : at + 2] + crossed[at + 2 : at + 3]
            back = jnp.concatenate([crossed[:SPAN], tall_rows(norm_row)], axis=0)
            back_ref[k, c] = back
            inner_ref[k, c] = crossed[SPAN:at]
            d_map = map_grad(up_ref[k, c], low_ref[k, c], d_feat[:width], d_feat[width:], 0)
            now = []
            for h in range(group):
                queries = q_ref[rows, (i * group + h) * width : (i * group + h + 1) * width]
                now.append(dot(d_map[:, h * SPAN : (h + 1) * SPAN], queries, NN))
            grads = now if grads is None else [a + b for a, b in zip(grads, now)]
            mine = flag(start == start_first) * back
            head = mine if head is None else head + mine
        head_ref[k * tall : (k + 1) * tall] = head
        for h in range(half):
            at = slice((k * half + h) * width, (k * half + h + 1) * width)
            keep_ref[at] = jnp.transpose(jnp.where(core == 0, grads[h], grads[half + h]))
            send_ref[at] = jnp.transpose(jnp.where(core == 0, grads[half + h], grads[h]))


def last_kernel(part, count, hops, *refs):
    spans_ref, k_ref, v_ref, w_ref, back_ref, inner_ref = refs[:6]
    came = refs[6 : 6 + hops]
    gk_ref = refs[6 + hops]
    width = w_ref.shape[-1]
    tall = back_ref.shape[2]
    place = lax.axis_index("seq")
    first = place * count
    _, end_last = bounds(spans_ref, first + count - 1)
    for i in range(*part):
        k = i - part[0]
        cols = slice(i * width, (i + 1) * width)
        keys = k_ref[:, cols]
        up, low = soft_pair(dot(keys, w_ref[i], NN), -1)
        grads = []
        for c in range(count):
            _, end = bounds(spans_ref, first + c)
            state = None
            for n in range(hops):
                near = end_last > (place + (1 << n)) * count
                some = came[n][k * tall : (k + 1) * tall]
                some = flag(jnp.logical_and(near, end > first + count)) * some
                state = some if state is None else state + some
            for e in range(c + 1, count):
                state = state + flag(end > first + e) * back_ref[k, e]
            norm = state[SPAN : SPAN + 1].astype(BF16).astype(F32)
            vals = v_ref[c * SPAN : (c + 1) * SPAN, cols]
            grads.append(inner_ref[k, c] + dot(vals, state[:SPAN].astype(BF16), NN) + norm)
        d_feat = jnp.concatenate(grads, axis=0)
        d_map = map_grad(up, low, d_feat[:, :width], d_feat[:, width:], -1)
        gk_ref[k * width : (k + 1) * width] = dot(keys, d_map, TN)


def cost(flops, moved):
    return pl.CostEstimate(flops=int(flops), bytes_accessed=int(moved), transcendentals=0)


SMEM = pl.BlockSpec(memory_space=pltpu.SMEM)
LIMIT = 32 << 20
PER_MICRO = 1e9


def local_call(body, out_shape, micros, *args, spans=None):
    first = [] if spans is None else [spans]
    return pl.pallas_call(
        body,
        out_shape=out_shape,
        in_specs=[SMEM] * len(first) + [pl.BlockSpec(memory_space=pltpu.VMEM)] * len(args),
        compiler_params=pltpu.CompilerParams(vmem_limit_bytes=LIMIT),
        cost_estimate=cost(micros * PER_MICRO, 0),
    )(*first, *args)


def index_in(stage):
    place = jnp.int32(0)
    for k, (axis, bit) in enumerate(stage):
        place = place + (((lax.axis_index(axis) >> bit) & 1) << k)
    return place


def split_kernel(stage, layout, *refs):
    pieces = 1 << len(stage)
    outs = refs[len(refs) - pieces :]
    mine = index_in(stage)
    for m, out in enumerate(outs):
        at, used = 0, 0
        for addends, rows in layout:
            size = rows // pieces
            start = 0 if pieces == 1 else pl.multiple_of((mine ^ m) * size, PAD)
            total = refs[used][pl.ds(start, size), :]
            for ref in refs[used + 1 : used + addends]:
                total = total + ref[pl.ds(start, size), :]
            out[at : at + size] = total
            at, used = at + size, used + addends


def join_pieces_kernel(stage, layout, *refs):
    pieces = 1 << len(stage)
    out = refs[pieces]
    mine = index_in(stage)
    for m in range(pieces):
        at, base = 0, 0
        for _, rows in layout:
            size = rows // pieces
            start = pl.multiple_of(base + (mine ^ m) * size, PAD)
            out[pl.ds(start, size), :] = refs[m][at : at + size]
            at, base = at + size, base + rows


def rows_of(rows, width):
    return jax.ShapeDtypeStruct((rows, width), F32)


class Summer:
    def __init__(self, n_dp, n_seq):
        self.n_dp, self.n_seq = n_dp, n_seq
        bits = [("dp", b) for b in range(1, n_dp.bit_length() - 1)]
        seq = [("seq", b) for b in range(n_seq.bit_length() - 1)]
        rest = bits[:1] + seq[:1] + seq[1:] + bits[1:]
        self.core = [("dp", 0)]
        self.stages = [rest[k : k + 2] for k in range(0, len(rest), 2)]

    def send(self, x, stage, mask):
        d_mask = sum(1 << b for k, (a, b) in enumerate(stage) if a == "dp" and mask >> k & 1)
        s_mask = sum(1 << b for k, (a, b) in enumerate(stage) if a == "seq" and mask >> k & 1)
        perm = [
            (d * self.n_seq + s, (d ^ d_mask) * self.n_seq + (s ^ s_mask))
            for d in range(self.n_dp)
            for s in range(self.n_seq)
        ]
        return lax.ppermute(x, ("dp", "seq"), perm)

    def split(self, groups, stage):
        pieces = 1 << len(stage)
        layout = [(len(g), g[0].shape[0]) for g in groups]
        size = sum(rows for _, rows in layout) // pieces
        width = groups[0][0].shape[1]
        out = local_call(
            functools.partial(split_kernel, stage, layout),
            [rows_of(size, width)] * pieces,
            0.4,
            *[a for g in groups for a in g],
        )
        return out, layout

    def join(self, x, stage, layout):
        came = [x] + [self.send(x, stage, m) for m in range(1, 1 << len(stage))]
        total = sum(rows for _, rows in layout)
        return local_call(
            functools.partial(join_pieces_kernel, stage, layout),
            rows_of(total, x.shape[1]),
            0.4,
            *came,
        )

    def scatter(self, groups, stage, whole=WHOLE):
        rows = [g[0].shape[0] for g in groups]
        if sum(rows) > whole and min(rows) >> len(stage) >= PAD:
            out, layout = self.split(groups, stage)
        else:
            whole, layout = self.split(groups, [])
            out, layout = [whole[0]] * (1 << len(stage)), None
        return [[out[0]] + [self.send(out[m], stage, m) for m in range(1, len(out))]], layout

    def gather(self, x, stage, layout):
        return x if layout is None else self.join(x, stage, layout)


def assemble_kernel(heads, half, stage, layout, own_ref, came_ref, key_own, key_came, out_ref, key_ref):
    join_pieces_kernel(stage, layout, key_own, key_came, key_ref)
    mine = lax.axis_index("dp") & 1
    for side, ref in enumerate((own_ref, came_ref)):
        for i in range(heads):
            start = pl.multiple_of((2 * i + (mine ^ side)) * half, PAD)
            out_ref[pl.ds(start, half), :] = ref[i * half : (i + 1) * half]


def solution(mesh):
    n_dp, n_seq = mesh.shape["dp"], mesh.shape["seq"]

    def shards(queries, keys, values, targets, q_map, k_map, doc_spans):
        hq, hd = q_map.shape[0], q_map.shape[1]
        hk = k_map.shape[0]
        group = hq // hk
        rows = queries.shape[1]
        count = rows // SPAN
        feats = 2 * hd
        tall = SPAN + PAD
        coef = 2.0 / math.sqrt(n_dp * n_seq * rows * hd)
        most = (3 * n_seq * count) // 8
        before = min(n_seq - 1, -(-(most - 1) // count))
        hops = max(1, before.bit_length())
        q2, t2 = queries[0], targets[0]
        k2, v2 = keys[0], values[0]
        parts = [(0, hk // 2), (hk // 2, hk)]
        array = jax.ShapeDtypeStruct
        stack = rows // hd
        weights = jnp.pad(k_map, ((0, -hk % stack), (0, 0), (0, 0)))
        weights = [weights[i : i + stack].reshape(rows, hd) for i in range(0, hk, stack)]
        out = local_call(
            functools.partial(key_kernel, count, parts, hd),
            [array((hk, rows, feats), BF16), array((hk, count, tall, feats), F32)]
            + [rows_of((hi - lo) * tall, feats) for lo, hi in parts],
            3.0,
            jnp.concatenate([k2, v2] + weights, axis=1),
            spans=doc_spans,
        )
        feat_k, blocks, tails = out[0], out[1], out[2:]

        def shift(own, hop, reverse):
            step = -hop if reverse else hop
            ring = [(i, (i + step) % n_seq) for i in range(n_seq)]
            return lax.ppermute(own, "seq", ring)

        def join(own, got, hop, reverse):
            return local_call(
                functools.partial(join_kernel, count, hop, reverse),
                rows_of(*own.shape),
                0.6,
                own,
                got,
                spans=doc_spans,
            )

        def exchange(own, reverse, start=0):
            came = []
            for k in range(start, hops):
                came.append(shift(own, 1 << k, reverse))
                if k < hops - 1:
                    own = join(own, came[-1], 1 << k, reverse)
            return came

        def early(part):
            wide = lambda r, dtype: array((part[1] - part[0], count, r, group * SPAN), dtype)
            return local_call(
                functools.partial(early_kernel, part, count, group),
                [wide(hd, F32), wide(hd, F32), wide(feats, BF16), wide(hd, F32), wide(PAD, F32)]
                + [wide(hd, BF16)],
                1.5,
                q2,
                t2,
                v2,
                feat_k,
                q_map,
            )

        def late(part, ready, came):
            heads = part[1] - part[0]
            return local_call(
                functools.partial(late_kernel, part, count, group, hops, coef),
                [rows_of(heads * group * hd // 2, hd)] * 2
                + [rows_of(heads * tall, feats)]
                + [array((heads, count, tall, feats), F32), array((heads, count, SPAN, feats), F32)],
                6,
                q2,
                v2,
                feat_k,
                blocks,
                *ready,
                *came,
                spans=doc_spans,
            )

        def last(part, back, inner, came):
            return local_call(
                functools.partial(last_kernel, part, count, hops),
                rows_of((part[1] - part[0]) * hd, hd),
                0.5,
                k2,
                v2,
                k_map,
                back,
                inner,
                *came,
                spans=doc_spans,
            )

        total = Summer(n_dp, n_seq)
        came = [exchange(t, False) for t in tails]
        ready = [early(p) for p in parts]
        first = late(parts[0], ready[0], came[0])
        back_one = [shift(first[2], 1, True)]
        core_one = total.send(first[1], total.core, 1)
        second = late(parts[1], ready[1], came[1])
        core_one, *second = lax.optimization_barrier((core_one, *second))
        back_two = [shift(second[2], 1, True)]
        core_two = total.send(second[1], total.core, 1)
        groups, layout = total.scatter([[first[0], core_one], [second[0], core_two]], total.stages[0])
        layouts = [layout]
        ends = [
            join(own[2], back[0], 1, True) if hops > 1 else back[0]
            for own, back in ((first, back_one), (second, back_two))
        ]
        if hops > 1:
            back_two += exchange(ends[1], True, 1)
            back_one += exchange(ends[0], True, 1)
        groups, ends = lax.optimization_barrier((groups, ends))
        for stage in total.stages[1:]:
            groups, layout = total.scatter(groups, stage)
            layouts.append(layout)
        x = total.split(groups, [])[0][0]
        gk = [
            last(p, m[3], m[4], b)
            for p, m, b in zip(parts, (first, second), (back_one, back_two))
        ]
        out, core_layout = total.split([[g] for g in gk], total.core)
        extra = [[out[0], total.send(out[1], total.core, 1)]]
        extra, layout = total.scatter(extra, total.stages[0], 2 * WHOLE)
        extra_layouts = [layout]
        x, extra = lax.optimization_barrier((x, extra))
        for stage, layout in reversed(list(zip(total.stages, layouts))):
            x = total.gather(x, stage, layout)
        for stage in total.stages[1:]:
            extra, layout = total.scatter(extra, stage, 2 * WHOLE)
            extra_layouts.append(layout)
        extra = total.split(extra, [])[0][0]
        for stage, layout in reversed(list(zip(total.stages, extra_layouts))):
            extra = total.gather(extra, stage, layout)
        x, extra = lax.optimization_barrier((x, extra))
        halves = [x, total.send(x, total.core, 1), extra, total.send(extra, total.core, 1)]
        grad_q, grad_k = local_call(
            functools.partial(assemble_kernel, hk, group * hd // 2, total.core, core_layout),
            [rows_of(hq * hd, hd), rows_of(hk * hd, hd)],
            1.0,
            *halves,
        )
        return grad_q.reshape(hq, hd, hd), grad_k.reshape(hk, hd, hd)

    in_specs = (
        P("dp", "seq", None),
        P("dp", "seq", None),
        P("dp", "seq", None),
        P("dp", "seq", None),
        P(),
        P(),
        P("dp", None),
    )
    return jax.shard_map(
        shards, mesh=mesh, in_specs=in_specs, out_specs=(P(), P()), check_vma=False
    )
```

```python
import functools
import math

import jax
import jax.numpy as jnp
from jax import lax
from jax.experimental import pallas as pl
from jax.experimental.pallas import tpu as pltpu
from jax.sharding import PartitionSpec as P

SPAN = 128
PAD = 8
WHOLE = 128
F32 = jnp.float32
BF16 = jnp.bfloat16
NN = (((1,), (0,)), ((), ()))
NT = (((1,), (1,)), ((), ()))
TN = (((0,), (0,)), ((), ()))
TT = (((0,), (1,)), ((), ()))


def dot(left, right, dims):
    return lax.dot_general(left, right, dims, preferred_element_type=F32)


def bounds(spans_ref, block):
    start, end, place = jnp.int32(0), jnp.int32(0), jnp.int32(0)
    for d in range(spans_ref.shape[1]):
        after = place + spans_ref[0, d]
        inside = jnp.logical_and(block >= place, block < after)
        start = jnp.where(inside, place, start)
        end = jnp.where(inside, after, end)
        place = after
    return start, end


def flag(condition):
    return jnp.where(condition, jnp.float32(1.0), jnp.float32(0.0))


def soft_pair(mapped, axis):
    up = jnp.exp(mapped - jnp.max(mapped, axis, keepdims=True))
    low = jnp.exp(jnp.min(mapped, axis, keepdims=True) - mapped)
    up = up * (1.0 / jnp.sum(up, axis, keepdims=True))
    low = low * (1.0 / jnp.sum(low, axis, keepdims=True))
    return up, low


def map_grad(up, low, grad_up, grad_low, axis):
    first = up * (grad_up - jnp.sum(up * grad_up, axis, keepdims=True))
    second = low * (grad_low - jnp.sum(low * grad_low, axis, keepdims=True))
    return (first - second).astype(BF16)


def tall_rows(row):
    return jnp.broadcast_to(row, (PAD, row.shape[1]))


def key_kernel(count, parts, width, spans_ref, packed_ref, feat_ref, block_ref, *tail_refs):
    total = parts[-1][1] * width
    stack = packed_ref.shape[0] // width
    first = lax.axis_index("seq") * count
    starts = [bounds(spans_ref, first + c)[0] for c in range(count)]
    for (lo, hi), tail_ref in zip(parts, tail_refs):
        for i in range(lo, hi):
            cols = slice(i * width, (i + 1) * width)
            at = 2 * total + i // stack * width
            weight = packed_ref[i % stack * width : (i % stack + 1) * width, at : at + width]
            up, low = soft_pair(dot(packed_ref[:, cols], weight, NN), -1)
            feat = jnp.concatenate([up, low], axis=-1).astype(BF16)
            feat_ref[i] = feat
            tail = None
            for c in range(count):
                rows = slice(c * SPAN, (c + 1) * SPAN)
                vals = packed_ref[rows, total + i * width : total + (i + 1) * width]
                state = dot(vals, feat[rows], TN)
                norm = jnp.sum(feat[rows].astype(F32), axis=0, keepdims=True)
                both = jnp.concatenate([state, tall_rows(norm)], axis=0)
                block_ref[i, c] = both
                part = flag(starts[c] == starts[count - 1]) * both
                tail = part if tail is None else tail + part
            tall = tail.shape[0]
            tail_ref[(i - lo) * tall : (i - lo + 1) * tall] = tail


def join_kernel(count, hop, reverse, spans_ref, own_ref, came_ref, out_ref):
    place = lax.axis_index("seq")
    if reverse:
        _, end = bounds(spans_ref, place * count)
        keep = flag(end > (place + hop) * count)
    else:
        start, _ = bounds(spans_ref, place * count + count - 1)
        keep = flag(start < (place - hop + 1) * count)
    out_ref[...] = own_ref[...] + keep * came_ref[...]


def causal_mask(columns):
    t = lax.broadcasted_iota(jnp.int32, (SPAN, columns), 1) & (SPAN - 1)
    return lax.broadcasted_iota(jnp.int32, (SPAN, columns), 0) <= t


def early_kernel(part, count, group, *refs):
    q_ref, t_ref, v_ref, feat_k_ref, w_ref = refs[:5]
    up_ref, low_ref, feat_ref, num_ref, den_ref, tgt_ref = refs[5:]
    width = w_ref.shape[-1]
    causal = causal_mask(group * SPAN)
    for i in range(*part):
        k = i - part[0]
        for c in range(count):
            rows = slice(c * SPAN, (c + 1) * SPAN)
            cols = [slice(h * width, (h + 1) * width) for h in range(i * group, (i + 1) * group)]
            mapped = [dot(w_ref[i * group + h], q_ref[rows, cols[h]], TT) for h in range(group)]
            up, low = soft_pair(jnp.concatenate(mapped, axis=1), 0)
            up_ref[k, c] = up
            low_ref[k, c] = low
            feat = jnp.concatenate([up, low], axis=0).astype(BF16)
            feat_ref[k, c] = feat
            scores = jnp.where(causal, dot(feat_k_ref[i, rows], feat, NN), 0.0)
            den_ref[k, c] = tall_rows(jnp.sum(scores, 0, keepdims=True))
            vals = v_ref[rows, i * width : (i + 1) * width]
            num_ref[k, c] = dot(vals, scores.astype(BF16), TN)
            for h in range(group):
                tgt_ref[k, c, :, h * SPAN : (h + 1) * SPAN] = jnp.transpose(t_ref[rows, cols[h]])


def late_kernel(part, count, group, hops, coef, *refs):
    spans_ref, q_ref, v_ref, feat_k_ref, block_ref = refs[:5]
    up_ref, low_ref, feat_ref, num_ref, den_ref, tgt_ref = refs[5:11]
    came = refs[11 : 11 + hops]
    keep_ref, send_ref, head_ref, back_ref, inner_ref = refs[11 + hops :]
    width = tgt_ref.shape[2]
    tall = block_ref.shape[2]
    half = group // 2
    core = lax.axis_index("dp") & 1
    place = lax.axis_index("seq")
    first = place * count
    start_first, _ = bounds(spans_ref, first)
    causal = causal_mask(group * SPAN)
    for i in range(*part):
        k = i - part[0]
        grads, head = None, None
        for c in range(count):
            rows = slice(c * SPAN, (c + 1) * SPAN)
            start, _ = bounds(spans_ref, first + c)
            state = None
            for n in range(hops):
                near = start_first < (place - (1 << n) + 1) * count
                some = came[n][k * tall : (k + 1) * tall]
                some = flag(jnp.logical_and(near, start < first)) * some
                state = some if state is None else state + some
            for e in range(c):
                state = state + flag(start <= first + e) * block_ref[i, e]
            state = jnp.concatenate([state, state[SPAN:]], axis=0).astype(BF16)
            feat_k = feat_k_ref[i, rows]
            feat = feat_ref[k, c]
            across = dot(state, feat, NN)
            numer = num_ref[k, c] + across[:SPAN]
            inverse = 1.0 / (den_ref[k, c, :1] + across[SPAN : SPAN + 1])
            output = numer * inverse
            d_out = coef * (output - tgt_ref[k, c].astype(F32))
            d_numer = (d_out * inverse).astype(BF16)
            d_denom = -jnp.sum(d_out * output, 0, keepdims=True) * inverse
            vals = v_ref[rows, i * width : (i + 1) * width]
            pairs = jnp.where(causal, dot(vals, d_numer, NN) + d_denom, 0.0).astype(BF16)
            mat = jnp.concatenate([feat_k, state[:SPAN]], axis=0)
            norm = jnp.transpose(state[SPAN:].astype(F32))[:, :1]
            d_feat = dot(mat, jnp.concatenate([pairs, d_numer], axis=0), TN) + norm * d_denom
            high = d_denom.astype(BF16)
            rest = d_denom - high.astype(F32)
            mid = rest.astype(BF16)
            low = (rest - mid.astype(F32)).astype(BF16)
            three = [high.astype(F32), mid.astype(F32), low.astype(F32)]
            three.append(jnp.zeros((2 * PAD - 3, high.shape[1]), F32))
            three = jnp.concatenate(three, axis=0).astype(BF16)
            left = jnp.concatenate([d_numer, pairs, three], axis=0)
            crossed = dot(left, feat, NT)
            at = 2 * SPAN
            norm_row = crossed[at : at + 1] + crossed[at + 1 : at + 2] + crossed[at + 2 : at + 3]
            back = jnp.concatenate([crossed[:SPAN], tall_rows(norm_row)], axis=0)
            back_ref[k, c] = back
            inner_ref[k, c] = crossed[SPAN:at]
            d_map = map_grad(up_ref[k, c], low_ref[k, c], d_feat[:width], d_feat[width:], 0)
            now = []
            for h in range(group):
                queries = q_ref[rows, (i * group + h) * width : (i * group + h + 1) * width]
                now.append(dot(d_map[:, h * SPAN : (h + 1) * SPAN], queries, NN))
            grads = now if grads is None else [a + b for a, b in zip(grads, now)]
            mine = flag(start == start_first) * back
            head = mine if head is None else head + mine
        head_ref[k * tall : (k + 1) * tall] = head
        for h in range(half):
            at = slice((k * half + h) * width, (k * half + h + 1) * width)
            keep_ref[at] = jnp.transpose(jnp.where(core == 0, grads[h], grads[half + h]))
            send_ref[at] = jnp.transpose(jnp.where(core == 0, grads[half + h], grads[h]))


def last_kernel(part, count, hops, *refs):
    spans_ref, k_ref, v_ref, w_ref, back_ref, inner_ref = refs[:6]
    came = refs[6 : 6 + hops]
    gk_ref = refs[6 + hops]
    width = w_ref.shape[-1]
    tall = back_ref.shape[2]
    place = lax.axis_index("seq")
    first = place * count
    _, end_last = bounds(spans_ref, first + count - 1)
    for i in range(*part):
        k = i - part[0]
        cols = slice(i * width, (i + 1) * width)
        keys = k_ref[:, cols]
        up, low = soft_pair(dot(keys, w_ref[i], NN), -1)
        grads = []
        for c in range(count):
            _, end = bounds(spans_ref, first + c)
            state = None
            for n in range(hops):
                near = end_last > (place + (1 << n)) * count
                some = came[n][k * tall : (k + 1) * tall]
                some = flag(jnp.logical_and(near, end > first + count)) * some
                state = some if state is None else state + some
            for e in range(c + 1, count):
                state = state + flag(end > first + e) * back_ref[k, e]
            norm = state[SPAN : SPAN + 1].astype(BF16).astype(F32)
            vals = v_ref[c * SPAN : (c + 1) * SPAN, cols]
            grads.append(inner_ref[k, c] + dot(vals, state[:SPAN].astype(BF16), NN) + norm)
        d_feat = jnp.concatenate(grads, axis=0)
        d_map = map_grad(up, low, d_feat[:, :width], d_feat[:, width:], -1)
        gk_ref[k * width : (k + 1) * width] = dot(keys, d_map, TN)


def cost(flops, moved):
    return pl.CostEstimate(flops=int(flops), bytes_accessed=int(moved), transcendentals=0)


SMEM = pl.BlockSpec(memory_space=pltpu.SMEM)
LIMIT = 32 << 20
PER_MICRO = 1e9


def local_call(body, out_shape, micros, *args, spans=None):
    first = [] if spans is None else [spans]
    return pl.pallas_call(
        body,
        out_shape=out_shape,
        in_specs=[SMEM] * len(first) + [pl.BlockSpec(memory_space=pltpu.VMEM)] * len(args),
        compiler_params=pltpu.CompilerParams(vmem_limit_bytes=LIMIT),
        cost_estimate=cost(micros * PER_MICRO, 0),
    )(*first, *args)


def index_in(stage):
    place = jnp.int32(0)
    for k, (axis, bit) in enumerate(stage):
        place = place + (((lax.axis_index(axis) >> bit) & 1) << k)
    return place


def split_kernel(stage, layout, *refs):
    pieces = 1 << len(stage)
    outs = refs[len(refs) - pieces :]
    mine = index_in(stage)
    for m, out in enumerate(outs):
        at, used = 0, 0
        for addends, rows in layout:
            size = rows // pieces
            start = 0 if pieces == 1 else pl.multiple_of((mine ^ m) * size, PAD)
            total = refs[used][pl.ds(start, size), :]
            for ref in refs[used + 1 : used + addends]:
                total = total + ref[pl.ds(start, size), :]
            out[at : at + size] = total
            at, used = at + size, used + addends


def join_pieces_kernel(stage, layout, *refs):
    pieces = 1 << len(stage)
    out = refs[pieces]
    mine = index_in(stage)
    for m in range(pieces):
        at, base = 0, 0
        for _, rows in layout:
            size = rows // pieces
            start = pl.multiple_of(base + (mine ^ m) * size, PAD)
            out[pl.ds(start, size), :] = refs[m][at : at + size]
            at, base = at + size, base + rows


def rows_of(rows, width):
    return jax.ShapeDtypeStruct((rows, width), F32)


class Summer:
    def __init__(self, n_dp, n_seq):
        self.n_dp, self.n_seq = n_dp, n_seq
        bits = [("dp", b) for b in range(1, n_dp.bit_length() - 1)]
        seq = [("seq", b) for b in range(n_seq.bit_length() - 1)]
        rest = bits[:1] + seq[:1] + seq[1:] + bits[1:]
        self.core = [("dp", 0)]
        self.stages = [rest[k : k + 2] for k in range(0, len(rest), 2)]

    def send(self, x, stage, mask):
        d_mask = sum(1 << b for k, (a, b) in enumerate(stage) if a == "dp" and mask >> k & 1)
        s_mask = sum(1 << b for k, (a, b) in enumerate(stage) if a == "seq" and mask >> k & 1)
        perm = [
            (d * self.n_seq + s, (d ^ d_mask) * self.n_seq + (s ^ s_mask))
            for d in range(self.n_dp)
            for s in range(self.n_seq)
        ]
        return lax.ppermute(x, ("dp", "seq"), perm)

    def split(self, groups, stage):
        pieces = 1 << len(stage)
        layout = [(len(g), g[0].shape[0]) for g in groups]
        size = sum(rows for _, rows in layout) // pieces
        width = groups[0][0].shape[1]
        out = local_call(
            functools.partial(split_kernel, stage, layout),
            [rows_of(size, width)] * pieces,
            0.15,
            *[a for g in groups for a in g],
        )
        return out, layout

    def join(self, x, stage, layout):
        came = [x] + [self.send(x, stage, m) for m in range(1, 1 << len(stage))]
        total = sum(rows for _, rows in layout)
        return local_call(
            functools.partial(join_pieces_kernel, stage, layout),
            rows_of(total, x.shape[1]),
            0.15,
            *came,
        )

    def scatter(self, groups, stage, whole=WHOLE):
        rows = [g[0].shape[0] for g in groups]
        if sum(rows) > whole and min(rows) >> len(stage) >= PAD:
            out, layout = self.split(groups, stage)
        else:
            whole, layout = self.split(groups, [])
            out, layout = [whole[0]] * (1 << len(stage)), None
        return [[out[0]] + [self.send(out[m], stage, m) for m in range(1, len(out))]], layout

    def gather(self, x, stage, layout):
        return x if layout is None else self.join(x, stage, layout)


def after(x, *others):
    return lax.optimization_barrier((x, others))[0]


def assemble_kernel(parts, half, stage, core, key_layout, *refs):
    pieces = 1 << len(stage)
    sides = (refs[:pieces], refs[pieces : 2 * pieces])
    key_own, key_came, out_ref, key_ref = refs[2 * pieces :]
    join_pieces_kernel(core, key_layout, key_own, key_came, key_ref)
    mine = index_in(stage)
    mine_core = index_in(core)
    for side, held in enumerate(sides):
        for m, ref in enumerate(held):
            at = 0
            for low, high in parts:
                size = (high - low) * half // pieces
                step = math.gcd(size, half)
                for k in range(0, size, step):
                    flat = (mine ^ m) * size + k
                    head = low + lax.div(flat, jnp.int32(half))
                    row = (2 * head + (mine_core ^ side)) * half + lax.rem(flat, jnp.int32(half))
                    out_ref[pl.ds(pl.multiple_of(row, PAD), step), :] = ref[at + k : at + k + step]
                at += size


def solution(mesh):
    n_dp, n_seq = mesh.shape["dp"], mesh.shape["seq"]

    def shards(queries, keys, values, targets, q_map, k_map, doc_spans):
        hq, hd = q_map.shape[0], q_map.shape[1]
        hk = k_map.shape[0]
        group = hq // hk
        rows = queries.shape[1]
        count = rows // SPAN
        feats = 2 * hd
        tall = SPAN + PAD
        coef = 2.0 / math.sqrt(n_dp * n_seq * rows * hd)
        most = (3 * n_seq * count) // 8
        before = min(n_seq - 1, -(-(most - 1) // count))
        hops = max(1, before.bit_length())
        q2, t2 = queries[0], targets[0]
        k2, v2 = keys[0], values[0]
        parts = [(0, hk // 2), (hk // 2, hk)]
        array = jax.ShapeDtypeStruct
        stack = rows // hd
        weights = jnp.pad(k_map, ((0, -hk % stack), (0, 0), (0, 0)))
        weights = [weights[i : i + stack].reshape(rows, hd) for i in range(0, hk, stack)]
        out = local_call(
            functools.partial(key_kernel, count, parts, hd),
            [array((hk, rows, feats), BF16), array((hk, count, tall, feats), F32)]
            + [rows_of((hi - lo) * tall, feats) for lo, hi in parts],
            3.0,
            jnp.concatenate([k2, v2] + weights, axis=1),
            spans=doc_spans,
        )
        feat_k, blocks, tails = out[0], out[1], out[2:]

        def shift(own, hop, reverse):
            step = -hop if reverse else hop
            ring = [(i, (i + step) % n_seq) for i in range(n_seq)]
            return lax.ppermute(own, "seq", ring)

        def join(own, got, hop, reverse):
            return local_call(
                functools.partial(join_kernel, count, hop, reverse),
                rows_of(*own.shape),
                0.6,
                own,
                got,
                spans=doc_spans,
            )

        def exchange(own, reverse, start=0):
            came = []
            for k in range(start, hops):
                came.append(shift(own, 1 << k, reverse))
                if k < hops - 1:
                    own = join(own, came[-1], 1 << k, reverse)
            return came

        def early(part):
            wide = lambda r, dtype: array((part[1] - part[0], count, r, group * SPAN), dtype)
            return local_call(
                functools.partial(early_kernel, part, count, group),
                [wide(hd, F32), wide(hd, F32), wide(feats, BF16), wide(hd, F32), wide(PAD, F32)]
                + [wide(hd, BF16)],
                1.5,
                q2,
                t2,
                v2,
                feat_k,
                q_map,
            )

        def late(part, ready, came):
            heads = part[1] - part[0]
            return local_call(
                functools.partial(late_kernel, part, count, group, hops, coef),
                [rows_of(heads * group * hd // 2, hd)] * 2
                + [rows_of(heads * tall, feats)]
                + [array((heads, count, tall, feats), F32), array((heads, count, SPAN, feats), F32)],
                6,
                q2,
                v2,
                feat_k,
                blocks,
                *ready,
                *came,
                spans=doc_spans,
            )

        def last(part, back, inner, came):
            return local_call(
                functools.partial(last_kernel, part, count, hops),
                rows_of((part[1] - part[0]) * hd, hd),
                0.5,
                k2,
                v2,
                k_map,
                back,
                inner,
                *came,
                spans=doc_spans,
            )

        total = Summer(n_dp, n_seq)
        came = [exchange(t, False) for t in tails]
        ready = [early(p) for p in parts]
        first = late(parts[0], ready[0], came[0])
        back_one = [shift(first[2], 1, True)]
        core_one = total.send(first[1], total.core, 1)
        second = late(parts[1], ready[1], came[1])
        core_one, *second = lax.optimization_barrier((core_one, *second))
        back_two = [shift(second[2], 1, True)]
        core_two = total.send(second[1], total.core, 1)
        groups, layout = total.scatter([[first[0], core_one], [second[0], core_two]], total.stages[0])
        layouts = [layout]
        ends = [
            join(own[2], back[0], 1, True) if hops > 1 else back[0]
            for own, back in ((first, back_one), (second, back_two))
        ]
        if hops > 1:
            back_two += exchange(ends[1], True, 1)
            back_one += exchange(ends[0], True, 1)
        groups, ends = lax.optimization_barrier((groups, ends))
        for stage in total.stages[1:]:
            groups, layout = total.scatter(groups, stage)
            layouts.append(layout)
        x = total.split(groups, [])[0][0]
        gk = [
            last(p, m[3], m[4], b)
            for p, m, b in zip(parts, (first, second), (back_one, back_two))
        ]
        out, core_layout = total.split([[g] for g in gk], total.core)
        extra = [[out[0], total.send(out[1], total.core, 1)]]
        extra, layout = total.scatter(extra, total.stages[0], 2 * WHOLE)
        extra_layouts = [layout]
        x, extra = lax.optimization_barrier((x, extra))
        for stage, layout in reversed(list(zip(total.stages[1:], layouts[1:]))):
            x = total.gather(x, stage, layout)
        own = [x] + [total.send(x, total.stages[0], m) for m in range(1, 1 << len(total.stages[0]))]
        for stage in total.stages[1:]:
            extra, layout = total.scatter(extra, stage, 2 * WHOLE)
            extra_layouts.append(layout)
        extra = total.split(extra, [])[0][0]
        for stage, layout in reversed(list(zip(total.stages, extra_layouts))):
            extra = total.gather(extra, stage, layout)
        own, extra = lax.optimization_barrier((own, extra))
        other = [total.send(piece, total.core, 1) for piece in own]
        grad_q, grad_k = local_call(
            functools.partial(
                assemble_kernel, parts, group * hd // 2, total.stages[0], total.core, core_layout
            ),
            [rows_of(hq * hd, hd), rows_of(hk * hd, hd)],
            1.0,
            *own,
            *other,
            extra,
            total.send(extra, total.core, 1),
        )
        return grad_q.reshape(hq, hd, hd), grad_k.reshape(hk, hd, hd)

    in_specs = (
        P("dp", "seq", None),
        P("dp", "seq", None),
        P("dp", "seq", None),
        P("dp", "seq", None),
        P(),
        P(),
        P("dp", None),
    )
    return jax.shard_map(
        shards, mesh=mesh, in_specs=in_specs, out_specs=(P(), P()), check_vma=False
    )
```

```python
import functools
import math

import jax
import jax.numpy as jnp
from jax import lax
from jax.experimental import pallas as pl
from jax.experimental.pallas import tpu as pltpu
from jax.sharding import PartitionSpec as P

SPAN = 128
PAD = 8
WHOLE = 128
F32 = jnp.float32
BF16 = jnp.bfloat16
NN = (((1,), (0,)), ((), ()))
NT = (((1,), (1,)), ((), ()))
TN = (((0,), (0,)), ((), ()))
TT = (((0,), (1,)), ((), ()))


def dot(left, right, dims):
    return lax.dot_general(left, right, dims, preferred_element_type=F32)


def bounds(spans_ref, block):
    start, end, place = jnp.int32(0), jnp.int32(0), jnp.int32(0)
    for d in range(spans_ref.shape[1]):
        after = place + spans_ref[0, d]
        inside = jnp.logical_and(block >= place, block < after)
        start = jnp.where(inside, place, start)
        end = jnp.where(inside, after, end)
        place = after
    return start, end


def flag(condition):
    return jnp.where(condition, jnp.float32(1.0), jnp.float32(0.0))


def soft_pair(mapped, axis):
    up = jnp.exp(mapped - jnp.max(mapped, axis, keepdims=True))
    low = jnp.exp(jnp.min(mapped, axis, keepdims=True) - mapped)
    up = up * (1.0 / jnp.sum(up, axis, keepdims=True))
    low = low * (1.0 / jnp.sum(low, axis, keepdims=True))
    return up, low


def map_grad(up, low, grad_up, grad_low, axis):
    first = up * (grad_up - jnp.sum(up * grad_up, axis, keepdims=True))
    second = low * (grad_low - jnp.sum(low * grad_low, axis, keepdims=True))
    return (first - second).astype(BF16)


def tall_rows(row):
    return jnp.broadcast_to(row, (PAD, row.shape[1]))


def key_kernel(count, parts, width, spans_ref, packed_ref, feat_ref, block_ref, *tail_refs):
    total = parts[-1][1] * width
    stack = packed_ref.shape[0] // width
    first = lax.axis_index("seq") * count
    starts = [bounds(spans_ref, first + c)[0] for c in range(count)]
    for (lo, hi), tail_ref in zip(parts, tail_refs):
        for i in range(lo, hi):
            cols = slice(i * width, (i + 1) * width)
            at = 2 * total + i // stack * width
            weight = packed_ref[i % stack * width : (i % stack + 1) * width, at : at + width]
            up, low = soft_pair(dot(packed_ref[:, cols], weight, NN), -1)
            feat = jnp.concatenate([up, low], axis=-1).astype(BF16)
            feat_ref[i] = feat
            tail = None
            for c in range(count):
                rows = slice(c * SPAN, (c + 1) * SPAN)
                vals = packed_ref[rows, total + i * width : total + (i + 1) * width]
                state = dot(vals, feat[rows], TN)
                norm = jnp.sum(feat[rows].astype(F32), axis=0, keepdims=True)
                both = jnp.concatenate([state, tall_rows(norm)], axis=0)
                if c < block_ref.shape[1]:
                    block_ref[i, c] = both
                part = flag(starts[c] == starts[count - 1]) * both
                tail = part if tail is None else tail + part
            tall = tail.shape[0]
            tail_ref[(i - lo) * tall : (i - lo + 1) * tall] = tail


def join_kernel(count, hop, reverse, spans_ref, own_ref, came_ref, out_ref):
    place = lax.axis_index("seq")
    if reverse:
        _, end = bounds(spans_ref, place * count)
        keep = flag(end > (place + hop) * count)
    else:
        start, _ = bounds(spans_ref, place * count + count - 1)
        keep = flag(start < (place - hop + 1) * count)
    out_ref[...] = own_ref[...] + keep * came_ref[...]


def causal_mask(columns):
    t = lax.broadcasted_iota(jnp.int32, (SPAN, columns), 1) & (SPAN - 1)
    return lax.broadcasted_iota(jnp.int32, (SPAN, columns), 0) <= t


def early_kernel(part, count, group, *refs):
    q_ref, t_ref, v_ref, feat_k_ref, w_ref = refs[:5]
    up_ref, low_ref, feat_ref, num_ref, den_ref, tgt_ref = refs[5:]
    width = w_ref.shape[-1]
    causal = causal_mask(group * SPAN)
    for i in range(*part):
        k = i - part[0]
        for c in range(count):
            rows = slice(c * SPAN, (c + 1) * SPAN)
            cols = [slice(h * width, (h + 1) * width) for h in range(i * group, (i + 1) * group)]
            mapped = [dot(w_ref[i * group + h], q_ref[rows, cols[h]], TT) for h in range(group)]
            up, low = soft_pair(jnp.concatenate(mapped, axis=1), 0)
            up_ref[k, c] = up
            low_ref[k, c] = low
            feat = jnp.concatenate([up, low], axis=0).astype(BF16)
            feat_ref[k, c] = feat
            scores = jnp.where(causal, dot(feat_k_ref[i, rows], feat, NN), 0.0)
            den_ref[k, c] = tall_rows(jnp.sum(scores, 0, keepdims=True))
            vals = v_ref[rows, i * width : (i + 1) * width]
            num_ref[k, c] = dot(vals, scores.astype(BF16), TN)
            for h in range(group):
                tgt_ref[k, c, :, h * SPAN : (h + 1) * SPAN] = jnp.transpose(t_ref[rows, cols[h]])


def late_kernel(part, count, group, hops, coef, *refs):
    spans_ref, q_ref, v_ref, feat_k_ref, block_ref = refs[:5]
    up_ref, low_ref, feat_ref, num_ref, den_ref, tgt_ref = refs[5:11]
    came = refs[11 : 11 + hops]
    keep_ref, send_ref, head_ref, back_ref, inner_ref = refs[11 + hops :]
    width = tgt_ref.shape[2]
    tall = block_ref.shape[2]
    half = group // 2
    core = lax.axis_index("dp") & 1
    place = lax.axis_index("seq")
    first = place * count
    start_first, _ = bounds(spans_ref, first)
    causal = causal_mask(group * SPAN)
    for i in range(*part):
        k = i - part[0]
        grads, head = None, None
        for c in range(count):
            rows = slice(c * SPAN, (c + 1) * SPAN)
            start, _ = bounds(spans_ref, first + c)
            state = None
            for n in range(hops):
                near = start_first < (place - (1 << n) + 1) * count
                some = came[n][k * tall : (k + 1) * tall]
                some = flag(jnp.logical_and(near, start < first)) * some
                state = some if state is None else state + some
            for e in range(c):
                state = state + flag(start <= first + e) * block_ref[i, e]
            state = jnp.concatenate([state, state[SPAN:]], axis=0).astype(BF16)
            feat_k = feat_k_ref[i, rows]
            feat = feat_ref[k, c]
            across = dot(state, feat, NN)
            numer = num_ref[k, c] + across[:SPAN]
            inverse = 1.0 / (den_ref[k, c, :1] + across[SPAN : SPAN + 1])
            output = numer * inverse
            d_out = coef * (output - tgt_ref[k, c].astype(F32))
            d_numer = (d_out * inverse).astype(BF16)
            d_denom = -jnp.sum(d_out * output, 0, keepdims=True) * inverse
            vals = v_ref[rows, i * width : (i + 1) * width]
            pairs = jnp.where(causal, dot(vals, d_numer, NN) + d_denom, 0.0).astype(BF16)
            mat = jnp.concatenate([feat_k, state[:SPAN]], axis=0)
            norm = jnp.transpose(state[SPAN:].astype(F32))[:, :1]
            d_feat = dot(mat, jnp.concatenate([pairs, d_numer], axis=0), TN) + norm * d_denom
            high = d_denom.astype(BF16)
            rest = d_denom - high.astype(F32)
            mid = rest.astype(BF16)
            low = (rest - mid.astype(F32)).astype(BF16)
            three = [high.astype(F32), mid.astype(F32), low.astype(F32)]
            three.append(jnp.zeros((2 * PAD - 3, high.shape[1]), F32))
            three = jnp.concatenate(three, axis=0).astype(BF16)
            left = jnp.concatenate([d_numer, pairs, three], axis=0)
            crossed = dot(left, feat, NT)
            at = 2 * SPAN
            norm_row = crossed[at : at + 1] + crossed[at + 1 : at + 2] + crossed[at + 2 : at + 3]
            back = jnp.concatenate([crossed[:SPAN], tall_rows(norm_row)], axis=0)
            back_ref[k, c] = back
            inner_ref[k, c] = crossed[SPAN:at]
            d_map = map_grad(up_ref[k, c], low_ref[k, c], d_feat[:width], d_feat[width:], 0)
            now = []
            for h in range(group):
                queries = q_ref[rows, (i * group + h) * width : (i * group + h + 1) * width]
                now.append(dot(d_map[:, h * SPAN : (h + 1) * SPAN], queries, NN))
            grads = now if grads is None else [a + b for a, b in zip(grads, now)]
            mine = flag(start == start_first) * back
            head = mine if head is None else head + mine
        head_ref[k * tall : (k + 1) * tall] = head
        for h in range(half):
            at = slice((k * half + h) * width, (k * half + h + 1) * width)
            keep_ref[at] = jnp.transpose(jnp.where(core == 0, grads[h], grads[half + h]))
            send_ref[at] = jnp.transpose(jnp.where(core == 0, grads[half + h], grads[h]))


def last_kernel(part, count, hops, *refs):
    spans_ref, k_ref, v_ref, w_ref, back_ref, inner_ref = refs[:6]
    came = refs[6 : 6 + hops]
    gk_ref = refs[6 + hops]
    width = w_ref.shape[-1]
    tall = back_ref.shape[2]
    place = lax.axis_index("seq")
    first = place * count
    _, end_last = bounds(spans_ref, first + count - 1)
    for i in range(*part):
        k = i - part[0]
        cols = slice(i * width, (i + 1) * width)
        keys = k_ref[:, cols]
        up, low = soft_pair(dot(keys, w_ref[i], NN), -1)
        grads = []
        for c in range(count):
            _, end = bounds(spans_ref, first + c)
            state = None
            for n in range(hops):
                near = end_last > (place + (1 << n)) * count
                some = came[n][k * tall : (k + 1) * tall]
                some = flag(jnp.logical_and(near, end > first + count)) * some
                state = some if state is None else state + some
            for e in range(c + 1, count):
                state = state + flag(end > first + e) * back_ref[k, e]
            norm = state[SPAN : SPAN + 1].astype(BF16).astype(F32)
            vals = v_ref[c * SPAN : (c + 1) * SPAN, cols]
            grads.append(inner_ref[k, c] + dot(vals, state[:SPAN].astype(BF16), NN) + norm)
        d_feat = jnp.concatenate(grads, axis=0)
        d_map = map_grad(up, low, d_feat[:, :width], d_feat[:, width:], -1)
        gk_ref[k * width : (k + 1) * width] = dot(keys, d_map, TN)


def cost(flops, moved):
    return pl.CostEstimate(flops=int(flops), bytes_accessed=int(moved), transcendentals=0)


SMEM = pl.BlockSpec(memory_space=pltpu.SMEM)
LIMIT = 32 << 20
PER_MICRO = 1e9


def local_call(body, out_shape, micros, *args, spans=None):
    first = [] if spans is None else [spans]
    return pl.pallas_call(
        body,
        out_shape=out_shape,
        in_specs=[SMEM] * len(first) + [pl.BlockSpec(memory_space=pltpu.VMEM)] * len(args),
        compiler_params=pltpu.CompilerParams(vmem_limit_bytes=LIMIT),
        cost_estimate=cost(micros * PER_MICRO, 0),
    )(*first, *args)


def index_in(stage):
    place = jnp.int32(0)
    for k, (axis, bit) in enumerate(stage):
        place = place + (((lax.axis_index(axis) >> bit) & 1) << k)
    return place


def split_kernel(stage, layout, *refs):
    pieces = 1 << len(stage)
    outs = refs[len(refs) - pieces :]
    mine = index_in(stage)
    for m, out in enumerate(outs):
        at, used = 0, 0
        for addends, rows in layout:
            size = rows // pieces
            start = 0 if pieces == 1 else pl.multiple_of((mine ^ m) * size, PAD)
            total = refs[used][pl.ds(start, size), :]
            for ref in refs[used + 1 : used + addends]:
                total = total + ref[pl.ds(start, size), :]
            out[at : at + size] = total
            at, used = at + size, used + addends


def join_pieces_kernel(stage, layout, *refs):
    pieces = 1 << len(stage)
    out = refs[pieces]
    mine = index_in(stage)
    for m in range(pieces):
        at, base = 0, 0
        for _, rows in layout:
            size = rows // pieces
            start = pl.multiple_of(base + (mine ^ m) * size, PAD)
            out[pl.ds(start, size), :] = refs[m][at : at + size]
            at, base = at + size, base + rows


def rows_of(rows, width):
    return jax.ShapeDtypeStruct((rows, width), F32)


class Summer:
    def __init__(self, n_dp, n_seq):
        self.n_dp, self.n_seq = n_dp, n_seq
        bits = [("dp", b) for b in range(1, n_dp.bit_length() - 1)]
        seq = [("seq", b) for b in range(n_seq.bit_length() - 1)]
        rest = bits[:1] + seq[:1] + seq[1:] + bits[1:]
        self.core = [("dp", 0)]
        self.stages = [rest[k : k + 2] for k in range(0, len(rest), 2)]

    def send(self, x, stage, mask):
        d_mask = sum(1 << b for k, (a, b) in enumerate(stage) if a == "dp" and mask >> k & 1)
        s_mask = sum(1 << b for k, (a, b) in enumerate(stage) if a == "seq" and mask >> k & 1)
        perm = [
            (d * self.n_seq + s, (d ^ d_mask) * self.n_seq + (s ^ s_mask))
            for d in range(self.n_dp)
            for s in range(self.n_seq)
        ]
        return lax.ppermute(x, ("dp", "seq"), perm)

    def split(self, groups, stage):
        pieces = 1 << len(stage)
        layout = [(len(g), g[0].shape[0]) for g in groups]
        size = sum(rows for _, rows in layout) // pieces
        width = groups[0][0].shape[1]
        out = local_call(
            functools.partial(split_kernel, stage, layout),
            [rows_of(size, width)] * pieces,
            0.15,
            *[a for g in groups for a in g],
        )
        return out, layout

    def join(self, x, stage, layout):
        came = [x] + [self.send(x, stage, m) for m in range(1, 1 << len(stage))]
        total = sum(rows for _, rows in layout)
        return local_call(
            functools.partial(join_pieces_kernel, stage, layout),
            rows_of(total, x.shape[1]),
            0.15,
            *came,
        )

    def scatter(self, groups, stage, whole=WHOLE):
        rows = [g[0].shape[0] for g in groups]
        if sum(rows) > whole and min(rows) >> len(stage) >= PAD:
            out, layout = self.split(groups, stage)
        else:
            whole, layout = self.split(groups, [])
            out, layout = [whole[0]] * (1 << len(stage)), None
        return [[out[0]] + [self.send(out[m], stage, m) for m in range(1, len(out))]], layout

    def gather(self, x, stage, layout):
        return x if layout is None else self.join(x, stage, layout)


def after(x, *others):
    return lax.optimization_barrier((x, others))[0]


def assemble_kernel(parts, half, stage, core, key_layout, *refs):
    pieces = 1 << len(stage)
    sides = (refs[:pieces], refs[pieces : 2 * pieces])
    key_own, key_came, out_ref, key_ref = refs[2 * pieces :]
    join_pieces_kernel(core, key_layout, key_own, key_came, key_ref)
    mine = index_in(stage)
    mine_core = index_in(core)
    for side, held in enumerate(sides):
        for m, ref in enumerate(held):
            at = 0
            for low, high in parts:
                size = (high - low) * half // pieces
                step = math.gcd(size, half)
                for k in range(0, size, step):
                    flat = (mine ^ m) * size + k
                    head = low + lax.div(flat, jnp.int32(half))
                    row = (2 * head + (mine_core ^ side)) * half + lax.rem(flat, jnp.int32(half))
                    out_ref[pl.ds(pl.multiple_of(row, PAD), step), :] = ref[at + k : at + k + step]
                at += size


def solution(mesh):
    n_dp, n_seq = mesh.shape["dp"], mesh.shape["seq"]

    def shards(queries, keys, values, targets, q_map, k_map, doc_spans):
        hq, hd = q_map.shape[0], q_map.shape[1]
        hk = k_map.shape[0]
        group = hq // hk
        rows = queries.shape[1]
        count = rows // SPAN
        feats = 2 * hd
        tall = SPAN + PAD
        coef = 2.0 / math.sqrt(n_dp * n_seq * rows * hd)
        most = (3 * n_seq * count) // 8
        before = min(n_seq - 1, -(-(most - 1) // count))
        hops = max(1, before.bit_length())
        q2, t2 = queries[0], targets[0]
        k2, v2 = keys[0], values[0]
        parts = [(0, hk // 2), (hk // 2, hk)]
        array = jax.ShapeDtypeStruct
        stack = rows // hd
        weights = jnp.pad(k_map, ((0, -hk % stack), (0, 0), (0, 0)))
        weights = [weights[i : i + stack].reshape(rows, hd) for i in range(0, hk, stack)]
        out = local_call(
            functools.partial(key_kernel, count, parts, hd),
            [array((hk, rows, feats), BF16), array((hk, max(count - 1, 1), tall, feats), F32)]
            + [rows_of((hi - lo) * tall, feats) for lo, hi in parts],
            3.0,
            jnp.concatenate([k2, v2] + weights, axis=1),
            spans=doc_spans,
        )
        feat_k, blocks, tails = out[0], out[1], out[2:]

        def shift(own, hop, reverse):
            step = -hop if reverse else hop
            ring = [(i, (i + step) % n_seq) for i in range(n_seq)]
            return lax.ppermute(own, "seq", ring)

        def join(own, got, hop, reverse):
            return local_call(
                functools.partial(join_kernel, count, hop, reverse),
                rows_of(*own.shape),
                0.6,
                own,
                got,
                spans=doc_spans,
            )

        def exchange(own, reverse, start=0):
            came = []
            for k in range(start, hops):
                came.append(shift(own, 1 << k, reverse))
                if k < hops - 1:
                    own = join(own, came[-1], 1 << k, reverse)
            return came

        def early(part):
            wide = lambda r, dtype: array((part[1] - part[0], count, r, group * SPAN), dtype)
            return local_call(
                functools.partial(early_kernel, part, count, group),
                [wide(hd, F32), wide(hd, F32), wide(feats, BF16), wide(hd, F32), wide(PAD, F32)]
                + [wide(hd, BF16)],
                1.5,
                q2,
                t2,
                v2,
                feat_k,
                q_map,
            )

        def late(part, ready, came):
            heads = part[1] - part[0]
            return local_call(
                functools.partial(late_kernel, part, count, group, hops, coef),
                [rows_of(heads * group * hd // 2, hd)] * 2
                + [rows_of(heads * tall, feats)]
                + [array((heads, count, tall, feats), F32), array((heads, count, SPAN, feats), F32)],
                6,
                q2,
                v2,
                feat_k,
                blocks,
                *ready,
                *came,
                spans=doc_spans,
            )

        def last(part, back, inner, came):
            return local_call(
                functools.partial(last_kernel, part, count, hops),
                rows_of((part[1] - part[0]) * hd, hd),
                0.5,
                k2,
                v2,
                k_map,
                back,
                inner,
                *came,
                spans=doc_spans,
            )

        total = Summer(n_dp, n_seq)
        came = [exchange(t, False) for t in tails]
        ready = [early(p) for p in parts]
        first = late(parts[0], ready[0], came[0])
        back_one = [shift(first[2], 1, True)]
        core_one = total.send(first[1], total.core, 1)
        second = late(parts[1], ready[1], came[1])
        core_one, *second = lax.optimization_barrier((core_one, *second))
        back_two = [shift(second[2], 1, True)]
        core_two = total.send(second[1], total.core, 1)
        groups, layout = total.scatter([[first[0], core_one], [second[0], core_two]], total.stages[0])
        layouts = [layout]
        ends = [
            join(own[2], back[0], 1, True) if hops > 1 else back[0]
            for own, back in ((first, back_one), (second, back_two))
        ]
        if hops > 1:
            back_two += exchange(ends[1], True, 1)
            back_one += exchange(ends[0], True, 1)
        groups, ends = lax.optimization_barrier((groups, ends))
        for stage in total.stages[1:]:
            groups, layout = total.scatter(groups, stage)
            layouts.append(layout)
        x = total.split(groups, [])[0][0]
        gk = [
            last(p, m[3], m[4], b)
            for p, m, b in zip(parts, (first, second), (back_one, back_two))
        ]
        out, core_layout = total.split([[g] for g in gk], total.core)
        extra = [[out[0], total.send(out[1], total.core, 1)]]
        extra, layout = total.scatter(extra, total.stages[0], 2 * WHOLE)
        extra_layouts = [layout]
        x, extra = lax.optimization_barrier((x, extra))
        for stage, layout in reversed(list(zip(total.stages[1:], layouts[1:]))):
            x = total.gather(x, stage, layout)
        own = [x] + [total.send(x, total.stages[0], m) for m in range(1, 1 << len(total.stages[0]))]
        for stage in total.stages[1:]:
            extra, layout = total.scatter(extra, stage, 2 * WHOLE)
            extra_layouts.append(layout)
        extra = total.split(extra, [])[0][0]
        for stage, layout in reversed(list(zip(total.stages, extra_layouts))):
            extra = total.gather(extra, stage, layout)
        own, extra = lax.optimization_barrier((own, extra))
        other = [total.send(piece, total.core, 1) for piece in own]
        grad_q, grad_k = local_call(
            functools.partial(
                assemble_kernel, parts, group * hd // 2, total.stages[0], total.core, core_layout
            ),
            [rows_of(hq * hd, hd), rows_of(hk * hd, hd)],
            1.0,
            *own,
            *other,
            extra,
            total.send(extra, total.core, 1),
        )
        return grad_q.reshape(hq, hd, hd), grad_k.reshape(hk, hd, hd)

    in_specs = (
        P("dp", "seq", None),
        P("dp", "seq", None),
        P("dp", "seq", None),
        P("dp", "seq", None),
        P(),
        P(),
        P("dp", None),
    )
    return jax.shard_map(
        shards, mesh=mesh, in_specs=in_specs, out_specs=(P(), P()), check_vma=False
    )
```
